256 devices in a mesh: py: 8 (over z), px: 8 (over y, core), vert: 4 (over x).
Axes of the slice: x: 4, y: 4, z: 8, core: 2. Of those that a mesh axis runs over, the one named last changes fastest.
Arguments:
- warped_image: float32 [8, 3072, 3072], P('vert', 'py', 'px'), may hold values from -6 to 6
- variance: float32 [8, 3072, 3072], P('vert', 'py', 'px'), may hold values from 0.25 to 4
- kernel_factors: float32 [8, 2304, 246], P('vert', ('py', 'px')), may hold values from -1 to 1
- cell_source: int32 [8, 2304], P('vert', ('py', 'px')), may hold values from 0 to 2303, as said below
- coverage: int32 [8, 2304], P('vert', ('py', 'px')), may hold values 0 or 1
Outputs:
- coadd: float32 [3072, 3072], P(('py', 'vert'), 'px')
- weight_sum: float32 [3072, 3072], P(('py', 'vert'), 'px')
The draws below stay inside these ranges and needn't reach their ends.
Inputs may be any that keep to these rules, and one draw needn't show every extreme that they name: `cell_source`: for each visit every storage index of a kernel cell is named exactly once; storage indices s * 36 to s * 36 + 35 belong to storage owner s, and for each visit and patch every storage owner holds either none or exactly 6 of that patch's cells.
All inputs are finite; a program needn't handle non-finite values. No bound on the sum of `coverage` on one device may be relied on, other than what follows from the above.
Results may differ from the reference program's by a relative error of at most 0.000098.
Values sent between devices are 32-bit elements; how exact they have to be, the bound alone decides.
A program may use at most 64 MiB of HBM per device.

```python
import math
import jax
import jax.numpy as jnp
from jax import lax

TAPS = 41
RANK = 3
CELL = 64
HALF = 20
CPS = 6
CELLS_DEV = 36
CAP = 6
FACT = 246
VISITS = 8
KCELLS = 2304
NY = 3072
NX = 3072
N_PY = 8
N_PX = 8


def draw_cell_source(key, part):
    key = jax.random.fold_in(key, 11)
    patch_count = N_PY * N_PX
    group_count = CELLS_DEV // CAP

    def single_visit(visit_key):
        keys_all = jax.random.split(visit_key, 4)
        row_order = jax.random.permutation(keys_all[0], patch_count)
        owner_order = jax.random.permutation(keys_all[1], patch_count)
        offsets = jax.random.permutation(keys_all[2], patch_count)[:group_count]
        block_orders = jax.vmap(single_block)(jax.random.split(keys_all[3], patch_count))
        patch_ids = jnp.arange(patch_count)[:, None, None]
        group_ids = jnp.arange(group_count)[None, :, None]
        item_ids = jnp.arange(CAP)[None, None, :]
        owners = owner_order[(row_order[patch_ids] + offsets[group_ids]) % patch_count]
        owners = jnp.broadcast_to(owners, (patch_count, group_count, CAP))
        slot_ids = jnp.broadcast_to(group_ids * CAP + item_ids, (patch_count, group_count, CAP))
        stored = owners * CELLS_DEV + block_orders[owners, slot_ids]
        return stored.reshape(-1).astype(jnp.int32)

    def single_block(block_key):
        return jax.random.permutation(block_key, CELLS_DEV)
    return jax.vmap(single_visit)(jax.random.split(key, VISITS))


def with_ends(result, own_key, low, largest):
    extent = result.shape
    spot = [jax.random.randint(jax.random.fold_in(own_key, axis), (), 0, extent[axis]) for axis in range(len(extent))]
    result = result.at[tuple(spot)].set(low)
    longest = extent.index(max(extent))
    spot[longest] = (spot[longest] + 1) % extent[longest]
    return result.at[tuple(spot)].set(largest)


def block_scale(stream_key, shape, shards, least, high):
    factor_of = 1.0
    for position, blocks in shards:
        draws = jax.random.uniform(jax.random.fold_in(jax.random.fold_in(stream_key, 6), position), (blocks,), jnp.float32, least / len(shards), high / len(shards))
        factor_of = factor_of * jnp.repeat(jnp.exp(draws), shape[position] // blocks).reshape((-1,) + (1,) * (len(shape) - 1 - position))
    return factor_of


def centred(rng, shape, deviation, bound, shards=(), dtype=jnp.bfloat16):
    values = deviation * jax.random.normal(rng, shape, jnp.float32)
    if shards:
        values = values * block_scale(rng, shape, shards, -0.22, 0.18)
    return jnp.clip(values, -bound, bound).astype(dtype)


def setup_inputs(seed: int = 0) -> dict:
    streams_of = jax.random.split(jax.random.key(seed), 6)
    warped_image = centred(streams_of[0], (VISITS, NY, NX), 1.0, 6.0, ((0, 4), (1, 8), (2, 8)), jnp.float32)
    variance = jnp.clip(jnp.exp(math.log(4.0) - 2.7725887 * jax.random.uniform(streams_of[1], (VISITS, NY, NX), jnp.float32) ** block_scale(streams_of[1], (VISITS, NY, NX), ((0, 4), (1, 8), (2, 8)), -0.2, 0.2)), 0.25, 4.0)
    kernel_factors = centred(streams_of[2], (VISITS, KCELLS, FACT), TAPS ** -0.5, 1.0, ((0, 4), (1, 64)), jnp.float32)
    cell_source = draw_cell_source(jax.random.fold_in(streams_of[5], 71), 0)
    coverage = with_ends((jax.random.randint(streams_of[4], (VISITS, KCELLS), 0, 2) < 1).astype(jnp.int32), jax.random.fold_in(streams_of[4], 1), 0, 1)
    return {"warped_image": warped_image, "variance": variance, "kernel_factors": kernel_factors, "cell_source": cell_source, "coverage": coverage}


weight_floor = 0.5
highest = lax.Precision.HIGHEST


def band_table():
    shift_ids = jnp.arange(TAPS)[:, None, None]
    row_ids = jnp.arange(CELL)[None, :, None]
    col_ids = jnp.arange(CELL + 2 * HALF)[None, None, :]
    return (col_ids - row_ids == shift_ids).astype(jnp.float32)


def cell_windows(padded, rows_cells, cols_cells):
    height = rows_cells * CELL
    width = cols_cells * CELL
    span = 2 * HALF
    extended = jnp.pad(padded, ((0, CELL - span), (0, CELL - span)))
    upper = extended[:height].reshape(rows_cells, CELL, width + CELL)
    lower = extended[CELL:height + CELL].reshape(rows_cells, CELL, width + CELL)[:, :span]
    stripes = jnp.concatenate([upper, lower], axis=1)
    left = stripes[:, :, :width].reshape(rows_cells, CELL + span, cols_cells, CELL)
    right = stripes[:, :, CELL:width + CELL].reshape(rows_cells, CELL + span, cols_cells, CELL)[..., :span]
    tiles = jnp.concatenate([left, right], axis=3)
    return tiles.transpose(0, 2, 1, 3).reshape(rows_cells * cols_cells, CELL + span, CELL + span)


def convolve_cells(tiles, factors):
    shaped = factors.reshape(-1, RANK, 2, TAPS)
    table = band_table()
    row_bands = jnp.einsum('crs,sik->crik', shaped[:, :, 0], table, precision=highest)
    col_bands = jnp.einsum('crs,sjl->crjl', shaped[:, :, 1], table, precision=highest)
    partial_pass = jnp.einsum('crik,ckl->cril', row_bands, tiles, precision=highest)
    return jnp.einsum('cril,crjl->cij', partial_pass, col_bands, precision=highest)


def assemble(blocks, rows_cells, cols_cells):
    return blocks.reshape(rows_cells, cols_cells, CELL, CELL).transpose(0, 2, 1, 3).reshape(rows_cells * CELL, cols_cells * CELL)


def cell_order():
    cell_rows = jnp.arange(NY // CELL)[:, None]
    cell_cols = jnp.arange(NX // CELL)[None, :]
    patch_flat = (cell_rows // CPS) * N_PX + cell_cols // CPS
    inner = (cell_rows % CPS) * CPS + cell_cols % CPS
    return (patch_flat * CELLS_DEV + inner).reshape(-1).astype(jnp.int32)


def reference(warped_image, variance, kernel_factors, cell_source, coverage):
    order = cell_order()
    rows_cells = NY // CELL
    cols_cells = NX // CELL

    def one_visit(operands):
        image_one, factors_one, source_one, cover_one = operands
        padded = jnp.pad(image_one, HALF)
        tiles = cell_windows(padded, rows_cells, cols_cells)
        chosen = factors_one[source_one[order]]
        convolved = assemble(convolve_cells(tiles, chosen), rows_cells, cols_cells)
        cover = cover_one[order].reshape(rows_cells, cols_cells).astype(jnp.float32)
        cover_pixels = jnp.repeat(jnp.repeat(cover, CELL, axis=0), CELL, axis=1)
        return convolved, cover_pixels

    convolved, cover_pixels = lax.map(one_visit, (warped_image, kernel_factors, cell_source, coverage))
    weights = cover_pixels / variance
    numerator = jnp.sum(weights * convolved, axis=0)
    denominator = jnp.sum(weights, axis=0)
    weight_sum = jnp.maximum(denominator, weight_floor)
    coadd = numerator / weight_sum
    return coadd, weight_sum
```

```python
import jax
import jax.numpy as jnp
from jax import lax
from jax.experimental import pallas as pl
from jax.experimental.pallas import tpu as pltpu
from jax.sharding import PartitionSpec as P

TAPS = 41
RANK = 3
CELL = 64
HALF = 20
CPS = 6
SIDE = 384
CELLS = 36
PAD = 40
FACT = 246
BORDER = 24
ROWS = SIDE + 2 * BORDER
WINDOW = 80
SHARE = 96
CHUNK = 72
N_VERT = 4
N_LINE = 8

MESH = pl.DeviceIdType.MESH
f32 = jnp.float32
bf16 = jnp.bfloat16


def lanes(rows):
    return lax.broadcasted_iota(jnp.int32, (rows, 128), 1)


def turn(x, shift):
    shift = shift % 128
    return x if shift == 0 else pltpu.roll(x, shift, 1)


def split(x):
    high = x.astype(bf16)
    low = (x - high.astype(f32)).astype(bf16)
    return high, low


def kernel(
    img, var, fac, cs, cov,
    coadd, wsum,
    ext, zbuf, csb, sbuf, rbuf, taps, xs, xr, thi, tlo, weight, num, den, rnum, rden,
    local_sem, zsend, zrecv, csend, crecv, ssend, srecv, hsend, hrecv, xsend, xrecv,
    nsend, nrecv, dsend, drecv,
):
    a = lax.axis_index("py")
    b = lax.axis_index("px")
    x = lax.axis_index("vert")

    def at_py(d):
        return {"py": lax.rem(a + d, N_LINE)}

    def at_px(d):
        return {"px": lax.rem(b + d, N_LINE)}

    def remote(src, dst, send, recv, device):
        return pltpu.make_async_remote_copy(
            src_ref=src, dst_ref=dst, send_sem=send, recv_sem=recv,
            device_id=device, device_id_type=MESH,
        )

    barrier = pltpu.get_barrier_semaphore()
    for d in (1, N_LINE - 1):
        pl.semaphore_signal(barrier, inc=1, device_id=at_py(d), device_id_type=MESH)
    for d in range(1, N_LINE):
        pl.semaphore_signal(barrier, inc=1, device_id=at_px(d), device_id_type=MESH)
    for d in range(1, N_VERT):
        pl.semaphore_signal(
            barrier, inc=1, device_id={"vert": lax.rem(x + d, N_VERT)}, device_id_type=MESH
        )

    own_image = pltpu.make_async_copy(img, ext.at[:, pl.ds(BORDER, SIDE), :], local_sem)
    own_image.start()

    for v in range(2):
        zbuf[v, 0] = jnp.zeros((PAD, 256), f32)
        zbuf[v, 0, 0:CELLS, 0:FACT] = fac[v]
        first = zbuf[v, 0, :, 0:128]
        second = zbuf[v, 0, :, 128:256]
        zbuf[v, 0, :, 128:256] = jnp.where(lanes(PAD) < 5, turn(first, 5), turn(second, 5))
    csb[0] = jnp.full((8, 128), -1.0, f32)
    csb[0, 0:2, 0:CELLS] = cs[...].astype(f32)

    pl.semaphore_wait(barrier, 2 + N_LINE - 1 + N_VERT - 1)

    cs_copies = [
        remote(csb.at[0], csb.at[N_LINE - d], csend.at[d], crecv.at[N_LINE - d], at_px(d))
        for d in range(1, N_LINE)
    ]

    def ring(v, source, target, d):
        return remote(
            zbuf.at[v, source], zbuf.at[v, target], zsend.at[v, target], zrecv.at[v, target],
            at_py(d),
        )

    up_chain = ((0, 1), (1, 2), (2, 3), (3, 4))
    down_chain = ((0, 7), (7, 6), (6, 5))
    z_up = [[ring(v, s, t, 1) for s, t in up_chain] for v in range(2)]
    z_down = [[ring(v, s, t, N_LINE - 1) for s, t in down_chain] for v in range(2)]
    h_down = remote(
        img.at[:, pl.ds(SIDE - BORDER, BORDER), :], ext.at[:, pl.ds(0, BORDER), :],
        hsend.at[0], hrecv.at[0], at_py(1),
    )
    h_up = remote(
        img.at[:, pl.ds(0, BORDER), :], ext.at[:, pl.ds(BORDER + SIDE, BORDER), :],
        hsend.at[1], hrecv.at[1], at_py(N_LINE - 1),
    )
    z_up[0][0].start()
    z_down[0][0].start()
    for copy in cs_copies:
        copy.start()
    z_up[1][0].start()
    z_down[1][0].start()
    h_down.start()
    h_up.start()

    def weight_rows(r, carry):
        rows = pl.ds(pl.multiple_of(r * CELL, CELL), CELL)
        lane = lanes(CELL)
        for c in range(CPS // 2):
            cols = pl.ds(128 * c, 128)
            total = jnp.zeros((CELL, 128), f32)
            for v in range(2):
                left = cov[v, r * CPS + 2 * c].astype(f32)
                right = cov[v, r * CPS + 2 * c + 1].astype(f32)
                w = jnp.where(lane < CELL, left, right) / var[v, rows, cols]
                weight[v, rows, cols] = w
                total = total + w
            den[rows, cols] = total
        return carry

    lax.fori_loop(0, CPS, weight_rows, 0)
    den_copies = []
    for d in range(1, N_VERT):
        target = lax.rem(x + d, N_VERT)
        den_copies.append(
            remote(
                den.at[pl.ds(pl.multiple_of(target * SHARE, SHARE), SHARE)], rden.at[d],
                dsend.at[d], drecv.at[d], {"vert": target},
            )
        )
        den_copies[-1].start()

    for step in range(1, 4):
        for v in range(2):
            z_up[v][step - 1].wait_recv()
            z_up[v][step].start()
            if step < 3:
                z_down[v][step - 1].wait_recv()
                z_down[v][step].start()

    own_image.wait()
    h_down.wait_recv()
    h_up.wait_recv()

    @pl.when(a == 0)
    def _():
        ext[:, 0:BORDER, :] = jnp.zeros((2, BORDER, SIDE), f32)

    @pl.when(a == N_LINE - 1)
    def _():
        ext[:, BORDER + SIDE:ROWS, :] = jnp.zeros((2, BORDER, SIDE), f32)

    def pack(v, carry):
        lane = lanes(CHUNK)
        last = jnp.zeros((CHUNK, 128), f32)
        first = jnp.zeros((CHUNK, 128), f32)
        for g in range(ROWS // CHUNK):
            inside = (lane >= HALF * g) & (lane < HALF * (g + 1))
            rows = slice(CHUNK * g, CHUNK * (g + 1))
            last = jnp.where(inside, turn(ext[v, rows, 256:384], HALF * g - 108), last)
            first = jnp.where(inside, turn(ext[v, rows, 0:128], HALF * g), first)
        xs[0, v] = last
        xs[1, v] = first
        return carry

    lax.fori_loop(0, 2, pack, 0)
    x_copies = [
        remote(xs.at[0], xr.at[0], xsend.at[0], xrecv.at[0], at_px(1)),
        remote(xs.at[1], xr.at[1], xsend.at[1], xrecv.at[1], at_px(N_LINE - 1)),
    ]
    for copy in x_copies:
        copy.start()

    for copy in cs_copies:
        copy.wait_recv()
    names = csb[...].reshape(8 * N_LINE, 128)
    wanted = jnp.concatenate([names, names], axis=0).T
    lane = lax.broadcasted_iota(jnp.int32, (1, 384), 1)
    behind = jnp.zeros((1, 384), jnp.int32)
    for n in range(1, N_LINE):
        behind = behind + (lane >= PAD * n).astype(jnp.int32)
    slot = lane - PAD * behind
    owner = (a - behind + N_LINE) & (N_LINE - 1)
    stored = ((owner * N_LINE + b) * CELLS + slot).astype(f32)
    stored = jnp.where(slot < CELLS, stored, -2.0)

    s_copies = [[None] * N_LINE for _ in range(2)]
    for v in range(2):
        z_up[v][3].wait_recv()
        z_down[v][2].wait_recv()
        high, low = split(zbuf[v].reshape(N_LINE * PAD, 256))
        table = jnp.concatenate([high, low], axis=1)
        table = jnp.concatenate([table, jnp.zeros((384 - N_LINE * PAD, 512), bf16)], axis=0)
        hot = jnp.concatenate(
            [
                jnp.where(wanted[0:PAD, 8 * d + v:8 * d + v + 1] == stored, 1.0, 0.0)
                for d in range(N_LINE)
            ],
            axis=0,
        ).astype(bf16)
        picked = jnp.dot(hot, table, preferred_element_type=f32)
        sbuf[v] = (picked[:, 0:256] + picked[:, 256:512]).reshape(N_LINE, PAD, 256)
        for d in range(1, N_LINE):
            s_copies[v][d] = remote(
                sbuf.at[v, d], rbuf.at[v, N_LINE - d], ssend.at[v, d],
                srecv.at[v, N_LINE - d], at_px(d),
            )
            s_copies[v][d].start()

    for copy in x_copies:
        copy.wait_recv()

    def tiles(v, carry):
        tall = 2 * CHUNK
        lane = lanes(tall)
        for j in range(ROWS // tall):
            rows = slice(tall * j, tall * (j + 1))
            raw = [ext[v, rows, 128 * d:128 * (d + 1)] for d in range(3)]
            even = [turn(t, HALF) for t in raw]
            odd = [turn(t, 84) for t in raw]
            border = xr[0, v]
            left = jnp.concatenate(
                [turn(border, -HALF * g) for g in (2 * j, 2 * j + 1)], axis=0
            )
            left = jnp.where(b == 0, 0.0, left)
            border = xr[1, v]
            right = jnp.concatenate(
                [turn(border, 84 - HALF * g) for g in (2 * j, 2 * j + 1)], axis=0
            )
            right = jnp.where(b == N_LINE - 1, 0.0, right)
            before = [left] + even
            after = odd + [right]
            for d in range(3):
                high, low = split(jnp.where(lane < HALF, before[d], even[d]))
                thi[v, 2 * d, rows] = high
                tlo[v, 2 * d, rows] = low
                high, low = split(jnp.where(lane < 84, odd[d], after[d + 1]))
                thi[v, 2 * d + 1, rows] = high
                tlo[v, 2 * d + 1, rows] = low
        return carry

    lax.fori_loop(0, 2, tiles, 0)

    for v in range(2):
        for d in range(1, N_LINE):
            s_copies[v][d].wait_recv()
        total = sbuf[v, 0]
        for d in range(1, N_LINE):
            total = total + rbuf[v, d]
        for p in range(2 * RANK):
            tile = total[:, 128 * (p // 3):128 * (p // 3 + 1)]
            tap = jnp.where(lanes(PAD) < TAPS, turn(tile, -TAPS * (p % 3)), 0.0)
            high = tap.astype(bf16).astype(f32)
            taps[v, p, 0] = high
            taps[v, p, 1] = tap - high

    def band(v, p, part, q, count, shift):
        row = jnp.broadcast_to(taps[v, p, part, pl.ds(q, 1), :], (count, 128))
        return pltpu.roll(row, shift, 1, stride=1, stride_axis=0)

    def convolve(v, r, c, q):
        half = CELL // 2
        lane = lanes(half)
        row_bands = []
        for k in range(RANK):
            near = band(v, 2 * k, 0, q, half, 4)
            low = band(v, 2 * k, 1, q, half, WINDOW + 4)
            far = band(v, 2 * k, 0, q, half, 2 * WINDOW + 4 - 128)
            row_bands.append(
                jnp.concatenate(
                    [
                        jnp.where(lane < WINDOW, near, low),
                        jnp.where(lane < 2 * WINDOW - 128, low, far),
                    ],
                    axis=1,
                )
            )
        row_bands = jnp.concatenate(row_bands, axis=0).astype(bf16)
        top = pl.multiple_of(r * CELL, CELL)
        windows = []
        for h in range(2):
            rows = pl.ds(pl.multiple_of(top + half * h, half), WINDOW)
            high = thi[v, c, rows, :]
            windows.append(
                jnp.concatenate([high, high, tlo[v, c, rows, :], high[0:16]], axis=0)
            )
        window = jnp.concatenate(windows, axis=1)
        partial_pass = jnp.dot(row_bands, window, preferred_element_type=f32)
        high, low = split(partial_pass)
        left = jnp.concatenate(
            [
                jnp.concatenate(
                    [
                        part[half * k:half * (k + 1), 128 * h:128 * (h + 1)]
                        for k in range(RANK)
                    ],
                    axis=1,
                )
                for part in (high, low)
                for h in range(2)
            ],
            axis=0,
        )
        col_bands = jnp.concatenate(
            [
                jnp.concatenate(
                    [band(v, 2 * k + 1, part, q, CELL, 0) for k in range(RANK)], axis=1
                )
                for part in range(2)
            ],
            axis=0,
        ).astype(bf16)
        both = lax.dot_general(
            left, col_bands, (((1,), (1,)), ((), ())), preferred_element_type=f32
        )
        both = both[0:CELL] + both[CELL:2 * CELL]
        return both + turn(both, CELL)

    def num_copy(t):
        d = lax.rem(t - x + N_VERT, N_VERT)
        return d, remote(
            num.at[pl.ds(SHARE * t, SHARE)], rnum.at[d], nsend.at[t], nrecv.at[d], {"vert": t}
        )

    def cell_row(r, carry):
        rows = pl.ds(pl.multiple_of(r * CELL, CELL), CELL)

        def cell_pair(c, carry):
            cols = pl.ds(pl.multiple_of(c * 128, 128), 128)
            total = jnp.zeros((CELL, 128), f32)
            for v in range(2):
                q = r * CPS + 2 * c
                one = convolve(v, r, 2 * c, q)
                two = convolve(v, r, 2 * c + 1, q + 1)
                total = total + weight[v, rows, cols] * jnp.where(lanes(CELL) < CELL, one, two)
            num[rows, cols] = total
            return carry

        lax.fori_loop(0, CPS // 2, cell_pair, 0)
        for t, ready in enumerate((1, 2, 4, 5)):
            d, copy = num_copy(t)

            @pl.when((r == ready) & (d != 0))
            def _():
                copy.start()

        return carry

    lax.fori_loop(0, CPS, cell_row, 0)

    mine = pl.ds(pl.multiple_of(x * SHARE, SHARE), SHARE)
    for copy in den_copies:
        copy.wait_recv()
    total = den[mine]
    for d in range(1, N_VERT):
        total = total + rden[d]
    total = jnp.maximum(total, 0.5)
    wsum[...] = total
    upper = num[mine]
    for d in range(1, N_VERT):
        remote(rnum.at[d], rnum.at[d], nsend.at[0], nrecv.at[d], {"vert": lax.rem(x + 1, N_VERT)}).wait_recv()
        upper = upper + rnum[d]
    coadd[...] = upper / total

    for t in range(N_VERT):
        d, copy = num_copy(t)

        @pl.when(d != 0)
        def _():
            copy.wait_send()

    for copy in den_copies + cs_copies + x_copies + [h_down, h_up]:
        copy.wait_send()
    for v in range(2):
        for copy in z_up[v] + z_down[v] + s_copies[v][1:]:
            copy.wait_send()


def shards(warped_image, variance, kernel_factors, cell_source, coverage):
    vmem = pl.BlockSpec(memory_space=pltpu.VMEM)
    dma = pltpu.SemaphoreType.DMA
    out = jax.ShapeDtypeStruct((SHARE, SIDE), f32)
    return pl.pallas_call(
        kernel,
        out_shape=(out, out),
        in_specs=[
            pl.BlockSpec(memory_space=pl.ANY), vmem, vmem, vmem,
            pl.BlockSpec(memory_space=pltpu.SMEM),
        ],
        out_specs=(vmem, vmem),
        scratch_shapes=[
            pltpu.VMEM((2, ROWS, SIDE), f32),
            pltpu.VMEM((2, N_LINE, PAD, 256), f32),
            pltpu.VMEM((N_LINE, 8, 128), f32),
            pltpu.VMEM((2, N_LINE, PAD, 256), f32),
            pltpu.VMEM((2, N_LINE, PAD, 256), f32),
            pltpu.VMEM((2, 2 * RANK, 2, PAD, 128), f32),
            pltpu.VMEM((2, 2, CHUNK, 128), f32),
            pltpu.VMEM((2, 2, CHUNK, 128), f32),
            pltpu.VMEM((2, CPS, ROWS, 128), bf16),
            pltpu.VMEM((2, CPS, ROWS, 128), bf16),
            pltpu.VMEM((2, SIDE, SIDE), f32),
            pltpu.VMEM((SIDE, SIDE), f32),
            pltpu.VMEM((SIDE, SIDE), f32),
            pltpu.VMEM((N_VERT, SHARE, SIDE), f32),
            pltpu.VMEM((N_VERT, SHARE, SIDE), f32),
            dma,
            dma((2, N_LINE)), dma((2, N_LINE)),
            dma((N_LINE,)), dma((N_LINE,)),
            dma((2, N_LINE)), dma((2, N_LINE)),
            dma((2,)), dma((2,)), dma((2,)), dma((2,)),
            dma((N_VERT,)), dma((N_VERT,)), dma((N_VERT,)), dma((N_VERT,)),
        ],
        compiler_params=pltpu.CompilerParams(
            collective_id=0, has_side_effects=True, vmem_limit_bytes=40 * 1024 * 1024
        ),
    )(warped_image, variance, kernel_factors, cell_source, coverage)


def solution(mesh):
    placed = (
        P("vert", "py", "px"),
        P("vert", "py", "px"),
        P("vert", ("py", "px"), None),
        P("vert", ("py", "px")),
        P("vert", ("py", "px")),
    )
    return jax.shard_map(
        shards,
        mesh=mesh,
        in_specs=placed,
        out_specs=(P(("py", "vert"), "px"), P(("py", "vert"), "px")),
        check_vma=False,
    )
```

```python
import jax
import jax.numpy as jnp
from jax import lax
from jax.experimental import pallas as pl
from jax.experimental.pallas import tpu as pltpu
from jax.sharding import PartitionSpec as P

TAPS = 41
RANK = 3
CELL = 64
HALF = 20
CPS = 6
SIDE = 384
CELLS = 36
PAD = 40
FACT = 246
BORDER = 24
ROWS = SIDE + 2 * BORDER
WINDOW = 80
SHARE = 96
CHUNK = 72
N_VERT = 4
N_LINE = 8

MESH = pl.DeviceIdType.MESH
f32 = jnp.float32
bf16 = jnp.bfloat16


def lanes(rows):
    return lax.broadcasted_iota(jnp.int32, (rows, 128), 1)


def turn(x, shift):
    shift = shift % 128
    return x if shift == 0 else pltpu.roll(x, shift, 1)


def split(x):
    high = x.astype(bf16)
    low = (x - high.astype(f32)).astype(bf16)
    return high, low


def kernel(
    img, var_in, fac_in, cs_in, cov_in,
    top_sum, weight_sum,
    ext, var, fac, cs, cov, zbuf, csb, hot, sbuf, rbuf, taps, xs, xr, thi, tlo, weight, num, den,
    rnum, rden, halves,
    in_sem, zsend, zrecv, csend, crecv, ssend, srecv, hsend, hrecv, xsend, xrecv,
    nsend, nrecv, dsend, drecv,
):
    a = lax.axis_index("py")
    b = lax.axis_index("px")
    x = lax.axis_index("vert")
    others = (lax.rem(x + 2, N_VERT), N_VERT - 1 - x, x + 1 - 2 * lax.rem(x, 2))

    def at_py(d):
        return {"py": lax.rem(a + d, N_LINE)}

    def at_px(d):
        return {"px": lax.rem(b + d, N_LINE)}

    def remote(src, dst, send, recv, device):
        return pltpu.make_async_remote_copy(
            src_ref=src, dst_ref=dst, send_sem=send, recv_sem=recv,
            device_id=device, device_id_type=MESH,
        )

    barrier = pltpu.get_barrier_semaphore()
    for d in range(1, N_LINE):
        pl.semaphore_signal(barrier, inc=1, device_id=at_py(d), device_id_type=MESH)
    for d in range(1, N_LINE):
        pl.semaphore_signal(barrier, inc=1, device_id=at_px(d), device_id_type=MESH)
    for target in others:
        pl.semaphore_signal(barrier, inc=1, device_id={"vert": target}, device_id_type=MESH)

    inputs = [
        pltpu.make_async_copy(source, target, in_sem.at[n])
        for n, (source, target) in enumerate((
            (fac_in, fac), (cs_in, cs), (cov_in, cov), (var_in, var),
            (img, ext.at[:, pl.ds(BORDER, SIDE), :]),
        ))
    ]
    for copy in inputs:
        copy.start()

    inputs[0].wait()
    for v in range(2):
        zbuf[v, 0] = jnp.zeros((PAD, 256), f32)
        zbuf[v, 0, 0:CELLS, 0:FACT] = fac[:, v, :]
    inputs[1].wait()
    csb[0] = jnp.full((8, 128), -1.0, f32)
    csb[0, 0:2, 0:CELLS] = cs[...].astype(f32)

    pl.semaphore_wait(barrier, 2 * (N_LINE - 1) + N_VERT - 1)

    def ring(v, source, target, d):
        return remote(
            zbuf.at[v, source], zbuf.at[v, target], zsend.at[v, target], zrecv.at[v, target],
            at_py(d),
        )

    z_first = [ring(0, 0, d, d) for d in (4, 3, 5, 2, 6, 1, 7)]
    z_up = [ring(1, s, t, 1) for s, t in ((0, 1), (1, 2), (2, 3), (3, 4))]
    z_down = [ring(1, s, t, N_LINE - 1) for s, t in ((0, 7), (7, 6), (6, 5))]
    cs_copies = [
        remote(csb.at[0], csb.at[N_LINE - d], csend.at[d], crecv.at[N_LINE - d], at_px(d))
        for d in range(1, N_LINE)
    ]
    h_down = remote(
        img.at[:, pl.ds(SIDE - BORDER, BORDER), :], ext.at[:, pl.ds(0, BORDER), :],
        hsend.at[0], hrecv.at[0], at_py(1),
    )
    h_up = remote(
        img.at[:, pl.ds(0, BORDER), :], ext.at[:, pl.ds(BORDER + SIDE, BORDER), :],
        hsend.at[1], hrecv.at[1], at_py(N_LINE - 1),
    )
    z_up[0].start()
    z_down[0].start()
    for copy in z_first + cs_copies + [h_down, h_up]:
        copy.start()

    def pass_on(step):
        z_up[step - 1].wait_recv()
        z_up[step].start()
        if step < 3:
            z_down[step - 1].wait_recv()
            z_down[step].start()

    inputs[2].wait()
    inputs[3].wait()

    def weight_rows(r, carry):
        rows = pl.ds(pl.multiple_of(r * CELL, CELL), CELL)
        lane = lanes(CELL)
        for c in range(CPS // 2):
            cols = pl.ds(128 * c, 128)
            total = jnp.zeros((CELL, 128), f32)
            for v in range(2):
                left = cov[v, r * CPS + 2 * c].astype(f32)
                right = cov[v, r * CPS + 2 * c + 1].astype(f32)
                w = jnp.where(lane < CELL, left, right) / var[v, rows, cols]
                weight[v, rows, cols] = w
                total = total + w
            den[rows, cols] = total
        return carry

    lax.fori_loop(0, CPS, weight_rows, 0)

    def share(ref, t):
        return ref.at[pl.ds(pl.multiple_of(t * SHARE, SHARE), SHARE)]

    den_copies = [
        remote(share(den, t), rden.at[n], dsend.at[n], drecv.at[n], {"vert": t})
        for n, t in enumerate(others)
    ]
    num_copies = [
        remote(share(num, t), rnum.at[n], nsend.at[n], nrecv.at[n], {"vert": t})
        for n, t in enumerate(others)
    ]
    for copy in den_copies:
        copy.start()
    pass_on(1)

    inputs[4].wait()
    h_down.wait_recv()
    h_up.wait_recv()

    @pl.when(a == 0)
    def _():
        ext[:, 0:BORDER, :] = jnp.zeros((2, BORDER, SIDE), f32)

    @pl.when(a == N_LINE - 1)
    def _():
        ext[:, BORDER + SIDE:ROWS, :] = jnp.zeros((2, BORDER, SIDE), f32)

    def pack(v, carry):
        lane = lanes(CHUNK)
        last = jnp.zeros((CHUNK, 128), f32)
        first = jnp.zeros((CHUNK, 128), f32)
        for g in range(ROWS // CHUNK):
            inside = (lane >= HALF * g) & (lane < HALF * (g + 1))
            rows = slice(CHUNK * g, CHUNK * (g + 1))
            last = jnp.where(inside, turn(ext[v, rows, 256:384], HALF * g - 108), last)
            first = jnp.where(inside, turn(ext[v, rows, 0:128], HALF * g), first)
        xs[0, v] = last
        xs[1, v] = first
        return carry

    lax.fori_loop(0, 2, pack, 0)
    x_copies = [
        remote(xs.at[0], xr.at[0], xsend.at[0], xrecv.at[0], at_px(1)),
        remote(xs.at[1], xr.at[1], xsend.at[1], xrecv.at[1], at_px(N_LINE - 1)),
    ]
    for copy in x_copies:
        copy.start()

    for copy in cs_copies:
        copy.wait_recv()
    names = csb[...].reshape(8 * N_LINE, 128)
    wanted = jnp.concatenate([names, names], axis=0).T
    lane = lax.broadcasted_iota(jnp.int32, (1, 384), 1)
    behind = jnp.zeros((1, 384), jnp.int32)
    for n in range(1, N_LINE):
        behind = behind + (lane >= PAD * n).astype(jnp.int32)
    slot = lane - PAD * behind
    owner = (a - behind + N_LINE) & (N_LINE - 1)
    stored = ((owner * N_LINE + b) * CELLS + slot).astype(f32)
    stored = jnp.where(slot < CELLS, stored, -2.0)
    for v in range(2):
        hot[v] = jnp.concatenate(
            [
                jnp.where(wanted[0:PAD, 8 * d + v:8 * d + v + 1] == stored, 1.0, 0.0)
                for d in range(N_LINE)
            ],
            axis=0,
        ).astype(bf16)
    pass_on(2)

    for copy in x_copies:
        copy.wait_recv()

    def tiles(v, carry):
        tall = 2 * CHUNK
        lane = lanes(tall)
        for j in range(ROWS // tall):
            rows = slice(tall * j, tall * (j + 1))
            raw = [ext[v, rows, 128 * d:128 * (d + 1)] for d in range(3)]
            even = [turn(t, HALF) for t in raw]
            odd = [turn(t, 84) for t in raw]
            border = xr[0, v]
            left = jnp.concatenate(
                [turn(border, -HALF * g) for g in (2 * j, 2 * j + 1)], axis=0
            )
            left = jnp.where(b == 0, 0.0, left)
            border = xr[1, v]
            right = jnp.concatenate(
                [turn(border, 84 - HALF * g) for g in (2 * j, 2 * j + 1)], axis=0
            )
            right = jnp.where(b == N_LINE - 1, 0.0, right)
            before = [left] + even
            after = odd + [right]
            for d in range(3):
                high, low = split(jnp.where(lane < HALF, before[d], even[d]))
                thi[v, 2 * d, rows] = high
                tlo[v, 2 * d, rows] = low
                high, low = split(jnp.where(lane < 84, odd[d], after[d + 1]))
                thi[v, 2 * d + 1, rows] = high
                tlo[v, 2 * d + 1, rows] = low
        return carry

    lax.fori_loop(0, 2, tiles, 0)
    pass_on(3)

    s_copies = [
        [
            remote(
                sbuf.at[v, d], rbuf.at[v, N_LINE - d], ssend.at[v, d],
                srecv.at[v, N_LINE - d], at_px(d),
            )
            for d in range(1, N_LINE)
        ]
        for v in range(2)
    ]
    for v, arrivals in ((0, z_first), (1, [z_up[3], z_down[2]])):
        for copy in arrivals:
            copy.wait_recv()
        high, low = split(zbuf[v].reshape(N_LINE * PAD, 256))
        table = jnp.concatenate([high, low], axis=1)
        table = jnp.concatenate([table, jnp.zeros((384 - N_LINE * PAD, 512), bf16)], axis=0)
        picked = jnp.dot(hot[v], table, preferred_element_type=f32)
        sbuf[v] = (picked[:, 0:256] + picked[:, 256:512]).reshape(N_LINE, PAD, 256)
        for copy in s_copies[v]:
            copy.start()

    half = CELL // 2

    def receive_taps(v):
        for copy in s_copies[v]:
            copy.wait_recv()
        total = sbuf[v, 0]
        for d in range(1, N_LINE):
            total = total + rbuf[v, d]
        lane = lanes(PAD)
        for p in range(2 * RANK):
            n, offset = divmod(TAPS * p, 128)
            tap = turn(total[:, 128 * n:128 * (n + 1)], -offset)
            if offset + TAPS > 128:
                rest = turn(total[:, 128 * (n + 1):128 * (n + 2)], -offset)
                tap = jnp.where(lane < 128 - offset, tap, rest)
            tap = jnp.where(lane < TAPS, tap, 0.0)
            high = tap.astype(bf16).astype(f32)
            taps[v, p, 0] = high
            taps[v, p, 1] = tap - high

    def band(v, p, part, q, count, shift):
        row = jnp.broadcast_to(taps[v, p, part, pl.ds(q, 1), :], (count, 128))
        return pltpu.roll(row, shift, 1, stride=1, stride_axis=0)

    def row_bands(v, q):
        lane = lanes(half)
        parts = []
        for k in range(RANK):
            near = band(v, 2 * k, 0, q, half, 4)
            low = band(v, 2 * k, 1, q, half, WINDOW + 4)
            far = band(v, 2 * k, 0, q, half, 2 * WINDOW + 4 - 128)
            parts.append(
                jnp.concatenate(
                    [
                        jnp.where(lane < WINDOW, near, low),
                        jnp.where(lane < 2 * WINDOW - 128, low, far),
                    ],
                    axis=1,
                )
            )
        return jnp.concatenate(parts, axis=0).astype(bf16)

    def col_bands(v, q):
        return jnp.concatenate(
            [
                jnp.concatenate(
                    [band(v, 2 * k + 1, part, q, CELL, 0) for k in range(RANK)], axis=1
                )
                for part in range(2)
            ],
            axis=0,
        ).astype(bf16)

    def row_of(step):
        late = step // 3
        place = step - 3 * late
        flip = lax.rem(x + late, 2)
        place = place + flip * (2 - 2 * place)
        side = x // 2
        return 3 * ((1 - side) * (1 - late) + side * late) + place

    def row_pass(v, step):
        r = row_of(step)
        top = pl.multiple_of(r * CELL, CELL)
        for c in range(CPS):
            windows = []
            for h in range(2):
                rows = pl.ds(pl.multiple_of(top + half * h, half), WINDOW)
                high = thi[v, c, rows, :]
                windows.append(
                    jnp.concatenate([high, high, tlo[v, c, rows, :], high[0:16]], axis=0)
                )
            part = jnp.dot(
                row_bands(v, r * CPS + c), jnp.concatenate(windows, axis=1),
                preferred_element_type=f32,
            )
            halves[lax.rem(step, 2) * CPS + c] = jnp.concatenate(
                [
                    jnp.concatenate(
                        [
                            piece[half * k:half * (k + 1), 128 * h:128 * (h + 1)]
                            for k in range(RANK)
                        ],
                        axis=1,
                    )
                    for piece in split(part)
                    for h in range(2)
                ],
                axis=0,
            )

    def col_pass(v, step):
        r = row_of(step)
        rows = pl.ds(pl.multiple_of(r * CELL, CELL), CELL)
        for c in range(0, CPS, 2):
            pair = []
            for n in (c, c + 1):
                both = lax.dot_general(
                    halves[lax.rem(step, 2) * CPS + n], col_bands(v, r * CPS + n),
                    (((1,), (1,)), ((), ())), preferred_element_type=f32,
                )
                both = both[0:CELL] + both[CELL:2 * CELL]
                pair.append(both + turn(both, CELL))
            cols = slice(CELL * c, CELL * c + 128)
            term = weight[v, rows, cols] * jnp.where(lanes(CELL) < CELL, pair[0], pair[1])
            num[rows, cols] = term if v == 0 else num[rows, cols] + term

    for v in range(2):
        receive_taps(v)
        row_pass(v, jnp.int32(0))

        def cell_row(step, carry):
            row_pass(v, step)
            col_pass(v, step - 1)
            if v == 1:
                for n, ready in enumerate((2, 3, 5)):

                    @pl.when(step == ready)
                    def _():
                        num_copies[n].start()

            return carry

        lax.fori_loop(1, CPS, cell_row, 0)
        col_pass(v, jnp.int32(CPS - 1))

    mine = pl.ds(pl.multiple_of(x * SHARE, SHARE), SHARE)
    for copy in den_copies + num_copies:
        copy.wait_recv()
    weight_sum[...] = (den[mine] + rden[1]) + (rden[0] + rden[2])
    top_sum[...] = (num[mine] + rnum[1]) + (rnum[0] + rnum[2])

    for copy in z_first + z_up + z_down + cs_copies + [h_down, h_up] + x_copies:
        copy.wait_send()
    for copy in s_copies[0] + s_copies[1] + den_copies + num_copies:
        copy.wait_send()


def shards(warped_image, variance, kernel_factors, cell_source, coverage):
    vmem = pl.BlockSpec(memory_space=pltpu.VMEM)
    dma = pltpu.SemaphoreType.DMA
    out = jax.ShapeDtypeStruct((SHARE, SIDE), f32)
    top_sum, weight_sum = pl.pallas_call(
        kernel,
        out_shape=(out, out),
        in_specs=[pl.BlockSpec(memory_space=pl.ANY)] * 5,
        out_specs=(vmem, vmem),
        scratch_shapes=[
            pltpu.VMEM((2, ROWS, SIDE), f32),
            pltpu.VMEM((2, SIDE, SIDE), f32),
            pltpu.VMEM((CELLS, 2, FACT), f32),
            pltpu.VMEM((2, CELLS), jnp.int32),
            pltpu.SMEM((2, CELLS), jnp.int32),
            pltpu.VMEM((2, N_LINE, PAD, 256), f32),
            pltpu.VMEM((N_LINE, 8, 128), f32),
            pltpu.VMEM((2, N_LINE * PAD, 384), bf16),
            pltpu.VMEM((2, N_LINE, PAD, 256), f32),
            pltpu.VMEM((2, N_LINE, PAD, 256), f32),
            pltpu.VMEM((2, 2 * RANK, 2, PAD, 128), f32),
            pltpu.VMEM((2, 2, CHUNK, 128), f32),
            pltpu.VMEM((2, 2, CHUNK, 128), f32),
            pltpu.VMEM((2, CPS, ROWS, 128), bf16),
            pltpu.VMEM((2, CPS, ROWS, 128), bf16),
            pltpu.VMEM((2, SIDE, SIDE), f32),
            pltpu.VMEM((SIDE, SIDE), f32),
            pltpu.VMEM((SIDE, SIDE), f32),
            pltpu.VMEM((N_VERT - 1, SHARE, SIDE), f32),
            pltpu.VMEM((N_VERT - 1, SHARE, SIDE), f32),
            pltpu.VMEM((2 * CPS, 128, 384), bf16),
            dma((5,)),
            dma((2, N_LINE)), dma((2, N_LINE)),
            dma((N_LINE,)), dma((N_LINE,)),
            dma((2, N_LINE)), dma((2, N_LINE)),
            dma((2,)), dma((2,)), dma((2,)), dma((2,)),
            dma((3,)), dma((3,)), dma((3,)), dma((3,)),
        ],
        compiler_params=pltpu.CompilerParams(
            collective_id=0, has_side_effects=True, vmem_limit_bytes=60 * 1024 * 1024
        ),
    )(warped_image, variance, kernel_factors.transpose(1, 0, 2), cell_source, coverage)
    weight_sum = jnp.maximum(weight_sum, 0.5)
    return top_sum / weight_sum, weight_sum


def solution(mesh):
    placed = (
        P("vert", "py", "px"),
        P("vert", "py", "px"),
        P("vert", ("py", "px"), None),
        P("vert", ("py", "px")),
        P("vert", ("py", "px")),
    )
    return jax.shard_map(
        shards,
        mesh=mesh,
        in_specs=placed,
        out_specs=(P(("py", "vert"), "px"), P(("py", "vert"), "px")),
        check_vma=False,
    )
```

```python
import jax
import jax.numpy as jnp
from jax import lax
from jax.experimental import pallas as pl
from jax.experimental.pallas import tpu as pltpu
from jax.sharding import PartitionSpec as P

TAPS = 41
RANK = 3
CELL = 64
HALF = 20
CPS = 6
SIDE = 384
CELLS = 36
PAD = 40
FACT = 246
BORDER = 24
ROWS = SIDE + 2 * BORDER
WINDOW = 80
SHARE = 96
EARLY = 16
CHUNK = 72
N_VERT = 4
N_LINE = 8

MESH = pl.DeviceIdType.MESH
f32 = jnp.float32
bf16 = jnp.bfloat16


def lanes(rows):
    return lax.broadcasted_iota(jnp.int32, (rows, 128), 1)


def turn(x, shift):
    shift = shift % 128
    return x if shift == 0 else pltpu.roll(x, shift, 1)


def split(x):
    high = x.astype(bf16)
    low = (x - high.astype(f32)).astype(bf16)
    return high, low


def kernel(
    img, var_in, fac_in, cs_in, cov_in,
    top_sum, weight_sum,
    ext, var, fac, cs, cov, zbuf, csb, hot, sbuf, rbuf, taps, xs, xr, thi, tlo, weight, num, den,
    rnum, rden, halves,
    in_sem, zsend, zrecv, csend, crecv, ssend, srecv, hsend, hrecv, xsend, xrecv,
    nsend, nrecv, dsend, drecv,
):
    a = lax.axis_index("py")
    b = lax.axis_index("px")
    x = lax.axis_index("vert")
    others = (lax.rem(x + 2, N_VERT), N_VERT - 1 - x, x + 1 - 2 * lax.rem(x, 2))

    def at_py(d):
        return {"py": lax.rem(a + d, N_LINE)}

    def at_px(d):
        return {"px": lax.rem(b + d, N_LINE)}

    def remote(src, dst, send, recv, device):
        return pltpu.make_async_remote_copy(
            src_ref=src, dst_ref=dst, send_sem=send, recv_sem=recv,
            device_id=device, device_id_type=MESH,
        )

    barrier = pltpu.get_barrier_semaphore()
    for d in range(1, N_LINE):
        pl.semaphore_signal(barrier, inc=1, device_id=at_py(d), device_id_type=MESH)
    for d in range(1, N_LINE):
        pl.semaphore_signal(barrier, inc=1, device_id=at_px(d), device_id_type=MESH)
    for target in others:
        pl.semaphore_signal(barrier, inc=1, device_id={"vert": target}, device_id_type=MESH)

    inputs = [
        pltpu.make_async_copy(source, target, in_sem.at[n])
        for n, (source, target) in enumerate((
            (fac_in, fac), (cs_in, cs), (cov_in, cov), (var_in, var),
            (img, ext.at[:, pl.ds(BORDER, SIDE), :]),
        ))
    ]
    for copy in inputs:
        copy.start()

    inputs[0].wait()
    for v in range(2):
        zbuf[v, 0] = jnp.zeros((PAD, 256), f32)
        zbuf[v, 0, 0:CELLS, 0:FACT] = fac[:, v, :]
    inputs[1].wait()
    csb[0] = jnp.full((8, 128), -1.0, f32)
    csb[0, 0:2, 0:CELLS] = cs[...].astype(f32)

    pl.semaphore_wait(barrier, 2 * (N_LINE - 1) + N_VERT - 1)

    def ring(v, source, target, d):
        return remote(
            zbuf.at[v, source], zbuf.at[v, target], zsend.at[v, target], zrecv.at[v, target],
            at_py(d),
        )

    z_first = [ring(0, 0, d, d) for d in (4, 3, 5, 2, 6, 1, 7)]
    z_up = [ring(1, s, t, 1) for s, t in ((0, 1), (1, 2), (2, 3), (3, 4))]
    z_down = [ring(1, s, t, N_LINE - 1) for s, t in ((0, 7), (7, 6), (6, 5))]
    cs_copies = [
        remote(csb.at[0], csb.at[N_LINE - d], csend.at[d], crecv.at[N_LINE - d], at_px(d))
        for d in range(1, N_LINE)
    ]
    h_down = remote(
        img.at[:, pl.ds(SIDE - BORDER, BORDER), :], ext.at[:, pl.ds(0, BORDER), :],
        hsend.at[0], hrecv.at[0], at_py(1),
    )
    h_up = remote(
        img.at[:, pl.ds(0, BORDER), :], ext.at[:, pl.ds(BORDER + SIDE, BORDER), :],
        hsend.at[1], hrecv.at[1], at_py(N_LINE - 1),
    )
    for copy in [h_down, h_up] + z_first + cs_copies + [z_up[0], z_down[0]]:
        copy.start()

    def pass_on(step):
        z_up[step - 1].wait_recv()
        z_up[step].start()
        if step < 3:
            z_down[step - 1].wait_recv()
            z_down[step].start()

    inputs[2].wait()
    inputs[3].wait()

    def weight_rows(r, carry):
        rows = pl.ds(pl.multiple_of(r * CELL, CELL), CELL)
        lane = lanes(CELL)
        for c in range(CPS // 2):
            cols = pl.ds(128 * c, 128)
            total = jnp.zeros((CELL, 128), f32)
            for v in range(2):
                left = cov[v, r * CPS + 2 * c].astype(f32)
                right = cov[v, r * CPS + 2 * c + 1].astype(f32)
                w = jnp.where(lane < CELL, left, right) / var[v, rows, cols]
                weight[v, rows, cols] = w
                total = total + w
            den[rows, cols] = total
        return carry

    lax.fori_loop(0, CPS, weight_rows, 0)

    def share(ref, t):
        return ref.at[pl.ds(pl.multiple_of(t * SHARE, SHARE), SHARE)]

    den_copies = [
        remote(share(den, t), rden.at[n], dsend.at[n], drecv.at[n], {"vert": t})
        for n, t in enumerate(others)
    ]
    for copy in den_copies:
        copy.start()

    def share_part(n, first, count, sem):
        t = others[n]
        first = first + lax.rem(t, 2) * (SHARE - count - 2 * first)
        first = pl.multiple_of(first, 32)
        base = pl.multiple_of(t * SHARE + first, 32)
        return remote(
            num.at[pl.ds(base, count)], rnum.at[n, pl.ds(first, count)],
            nsend.at[sem], nrecv.at[sem], {"vert": t},
        )

    inputs[4].wait()
    h_down.wait_recv()
    h_up.wait_recv()

    @pl.when(a == 0)
    def _():
        ext[:, 0:BORDER, :] = jnp.zeros((2, BORDER, SIDE), f32)

    @pl.when(a == N_LINE - 1)
    def _():
        ext[:, BORDER + SIDE:ROWS, :] = jnp.zeros((2, BORDER, SIDE), f32)

    def pack(v, carry):
        lane = lanes(CHUNK)
        last = jnp.zeros((CHUNK, 128), f32)
        first = jnp.zeros((CHUNK, 128), f32)
        for g in range(ROWS // CHUNK):
            inside = (lane >= HALF * g) & (lane < HALF * (g + 1))
            rows = slice(CHUNK * g, CHUNK * (g + 1))
            last = jnp.where(inside, turn(ext[v, rows, 256:384], HALF * g - 108), last)
            first = jnp.where(inside, turn(ext[v, rows, 0:128], HALF * g), first)
        xs[0, v] = last
        xs[1, v] = first
        return carry

    lax.fori_loop(0, 2, pack, 0)
    x_copies = [
        remote(xs.at[0], xr.at[0], xsend.at[0], xrecv.at[0], at_px(1)),
        remote(xs.at[1], xr.at[1], xsend.at[1], xrecv.at[1], at_px(N_LINE - 1)),
    ]
    for copy in x_copies:
        copy.start()

    pass_on(1)

    for copy in cs_copies:
        copy.wait_recv()
    names = csb[...].reshape(8 * N_LINE, 128)
    wanted = jnp.concatenate([names, names], axis=0).T
    lane = lax.broadcasted_iota(jnp.int32, (1, 384), 1)
    behind = jnp.zeros((1, 384), jnp.int32)
    for n in range(1, N_LINE):
        behind = behind + (lane >= PAD * n).astype(jnp.int32)
    slot = lane - PAD * behind
    owner = (a - behind + N_LINE) & (N_LINE - 1)
    stored = ((owner * N_LINE + b) * CELLS + slot).astype(f32)
    stored = jnp.where(slot < CELLS, stored, -2.0)
    for v in range(2):
        hot[v] = jnp.concatenate(
            [
                jnp.where(wanted[0:PAD, 8 * d + v:8 * d + v + 1] == stored, 1.0, 0.0)
                for d in range(N_LINE)
            ],
            axis=0,
        ).astype(bf16)
    pass_on(2)

    def pick_copies(v, first, count, sem):
        rows = pl.ds(first, count)
        return [
            remote(
                sbuf.at[v, d, rows], rbuf.at[v, N_LINE - d, rows], ssend.at[sem, d],
                srecv.at[sem, N_LINE - d], at_px(d),
            )
            for d in range(1, N_LINE)
        ]

    s_copies = [pick_copies(0, 0, EARLY, 0), pick_copies(0, EARLY, PAD - EARLY, 1), pick_copies(1, 0, PAD, 2)]

    def pick(v):
        high, low = split(zbuf[v].reshape(N_LINE * PAD, 256))
        table = jnp.concatenate([high, low], axis=1)
        table = jnp.concatenate([table, jnp.zeros((384 - N_LINE * PAD, 512), bf16)], axis=0)
        picked = jnp.dot(hot[v], table, preferred_element_type=f32)
        sbuf[v] = (picked[:, 0:256] + picked[:, 256:512]).reshape(N_LINE, PAD, 256)

    for copy in z_first:
        copy.wait_recv()
    pick(0)
    for copy in s_copies[0] + s_copies[1]:
        copy.start()
    pass_on(3)

    for copy in x_copies:
        copy.wait_recv()

    def tiles(v):
        tall = 2 * CHUNK
        lane = lanes(tall)
        for j in range(ROWS // tall):
            rows = slice(tall * j, tall * (j + 1))
            raw = [ext[v, rows, 128 * d:128 * (d + 1)] for d in range(3)]
            even = [turn(t, HALF) for t in raw]
            odd = [turn(t, 84) for t in raw]
            border = xr[0, v]
            left = jnp.concatenate(
                [turn(border, -HALF * g) for g in (2 * j, 2 * j + 1)], axis=0
            )
            left = jnp.where(b == 0, 0.0, left)
            border = xr[1, v]
            right = jnp.concatenate(
                [turn(border, 84 - HALF * g) for g in (2 * j, 2 * j + 1)], axis=0
            )
            right = jnp.where(b == N_LINE - 1, 0.0, right)
            before = [left] + even
            after = odd + [right]
            for d in range(3):
                high, low = split(jnp.where(lane < HALF, before[d], even[d]))
                thi[v, 2 * d, rows] = high
                tlo[v, 2 * d, rows] = low
                high, low = split(jnp.where(lane < 84, odd[d], after[d + 1]))
                thi[v, 2 * d + 1, rows] = high
                tlo[v, 2 * d + 1, rows] = low

    tiles(0)
    tiles(1)

    for copy in (z_up[3], z_down[2]):
        copy.wait_recv()
    pick(1)
    for copy in s_copies[2]:
        copy.start()

    half = CELL // 2

    def receive_taps(v, first, count, copies):
        for copy in copies:
            copy.wait_recv()
        rows = slice(first, first + count)
        total = sbuf[v, 0, rows]
        for d in range(1, N_LINE):
            total = total + rbuf[v, d, rows]
        lane = lanes(count)
        for p in range(2 * RANK):
            n, offset = divmod(TAPS * p, 128)
            tap = turn(total[:, 128 * n:128 * (n + 1)], -offset)
            if offset + TAPS > 128:
                rest = turn(total[:, 128 * (n + 1):128 * (n + 2)], -offset)
                tap = jnp.where(lane < 128 - offset, tap, rest)
            tap = jnp.where(lane < TAPS, tap, 0.0)
            high = tap.astype(bf16).astype(f32)
            taps[v, p, 0, rows] = high
            taps[v, p, 1, rows] = tap - high

    def band(v, p, part, q, count, shift):
        row = jnp.broadcast_to(taps[v, p, part, pl.ds(q, 1), :], (count, 128))
        return pltpu.roll(row, shift, 1, stride=1, stride_axis=0)

    def row_bands(v, q):
        lane = lanes(half)
        parts = []
        for k in range(RANK):
            near = band(v, 2 * k, 0, q, half, 4)
            low = band(v, 2 * k, 1, q, half, WINDOW + 4)
            far = band(v, 2 * k, 0, q, half, 2 * WINDOW + 4 - 128)
            parts.append(
                jnp.concatenate(
                    [
                        jnp.where(lane < WINDOW, near, low),
                        jnp.where(lane < 2 * WINDOW - 128, low, far),
                    ],
                    axis=1,
                )
            )
        return jnp.concatenate(parts, axis=0).astype(bf16)

    def col_bands(v, q):
        return jnp.concatenate(
            [
                jnp.concatenate(
                    [band(v, 2 * k + 1, part, q, CELL, 0) for k in range(RANK)], axis=1
                )
                for part in range(2)
            ],
            axis=0,
        ).astype(bf16)

    def row_of(v, step):
        if v == 0:
            return step
        late = step // 3
        place = step - 3 * late
        flip = lax.rem(x + late, 2)
        place = place + flip * (2 - 2 * place)
        side = x // 2
        return 3 * ((1 - side) * (1 - late) + side * late) + place

    def row_pass(v, step):
        r = row_of(v, step)
        top = pl.multiple_of(r * CELL, CELL)
        for c in range(CPS):
            windows = []
            for h in range(2):
                rows = pl.ds(pl.multiple_of(top + half * h, half), WINDOW)
                high = thi[v, c, rows, :]
                windows.append(
                    jnp.concatenate([high, high, tlo[v, c, rows, :], high[0:16]], axis=0)
                )
            part = jnp.dot(
                row_bands(v, r * CPS + c), jnp.concatenate(windows, axis=1),
                preferred_element_type=f32,
            )
            halves[lax.rem(step, 2) * CPS + c] = jnp.concatenate(
                [
                    jnp.concatenate(
                        [
                            piece[half * k:half * (k + 1), 128 * h:128 * (h + 1)]
                            for k in range(RANK)
                        ],
                        axis=1,
                    )
                    for piece in split(part)
                    for h in range(2)
                ],
                axis=0,
            )

    def col_pass(v, step):
        r = row_of(v, step)
        rows = pl.ds(pl.multiple_of(r * CELL, CELL), CELL)
        for c in range(0, CPS, 2):
            pair = []
            for n in (c, c + 1):
                both = lax.dot_general(
                    halves[lax.rem(step, 2) * CPS + n], col_bands(v, r * CPS + n),
                    (((1,), (1,)), ((), ())), preferred_element_type=f32,
                )
                both = both[0:CELL] + both[CELL:2 * CELL]
                pair.append(both + turn(both, CELL))
            cols = slice(CELL * c, CELL * c + 128)
            term = weight[v, rows, cols] * jnp.where(lanes(CELL) < CELL, pair[0], pair[1])
            num[rows, cols] = term if v == 0 else num[rows, cols] + term

    def cell_row(v, step):
        row_pass(v, step)
        col_pass(v, step - 1)

    receive_taps(0, 0, EARLY, s_copies[0])
    row_pass(0, jnp.int32(0))

    @pl.loop(1, EARLY // CPS)
    def _(step):
        cell_row(0, step)

    receive_taps(0, EARLY, PAD - EARLY, s_copies[1])

    @pl.loop(EARLY // CPS, CPS)
    def _(step):
        cell_row(0, step)

    col_pass(0, jnp.int32(CPS - 1))

    receive_taps(1, 0, PAD, s_copies[2])
    row_pass(1, jnp.int32(0))
    num_copies = [
        share_part(0, 0, 64, 0), share_part(0, 64, 32, 1), share_part(1, 0, 96, 2),
        share_part(2, 0, 64, 3), share_part(2, 64, 32, 4),
    ]

    @pl.loop(1, CPS)
    def _(step):
        cell_row(1, step)
        for n, copy in enumerate(num_copies):

            @pl.when(step == n + 1)
            def _():
                copy.start()

    col_pass(1, jnp.int32(CPS - 1))

    mine = pl.ds(pl.multiple_of(x * SHARE, SHARE), SHARE)
    for copy in den_copies + num_copies:
        copy.wait_recv()
    weight_sum[...] = (den[mine] + rden[1]) + (rden[0] + rden[2])
    top_sum[...] = (num[mine] + rnum[1]) + (rnum[0] + rnum[2])

    for copy in z_first + z_up + z_down + cs_copies + [h_down, h_up] + x_copies:
        copy.wait_send()
    for copy in s_copies[0] + s_copies[1] + s_copies[2] + den_copies + num_copies:
        copy.wait_send()


def shards(warped_image, variance, kernel_factors, cell_source, coverage):
    vmem = pl.BlockSpec(memory_space=pltpu.VMEM)
    dma = pltpu.SemaphoreType.DMA
    out = jax.ShapeDtypeStruct((SHARE, SIDE), f32)
    top_sum, weight_sum = pl.pallas_call(
        kernel,
        out_shape=(out, out),
        in_specs=[pl.BlockSpec(memory_space=pl.ANY)] * 5,
        out_specs=(vmem, vmem),
        scratch_shapes=[
            pltpu.VMEM((2, ROWS, SIDE), f32),
            pltpu.VMEM((2, SIDE, SIDE), f32),
            pltpu.VMEM((CELLS, 2, FACT), f32),
            pltpu.VMEM((2, CELLS), jnp.int32),
            pltpu.SMEM((2, CELLS), jnp.int32),
            pltpu.VMEM((2, N_LINE, PAD, 256), f32),
            pltpu.VMEM((N_LINE, 8, 128), f32),
            pltpu.VMEM((2, N_LINE * PAD, 384), bf16),
            pltpu.VMEM((2, N_LINE, PAD, 256), f32),
            pltpu.VMEM((2, N_LINE, PAD, 256), f32),
            pltpu.VMEM((2, 2 * RANK, 2, PAD, 128), f32),
            pltpu.VMEM((2, 2, CHUNK, 128), f32),
            pltpu.VMEM((2, 2, CHUNK, 128), f32),
            pltpu.VMEM((2, CPS, ROWS, 128), bf16),
            pltpu.VMEM((2, CPS, ROWS, 128), bf16),
            pltpu.VMEM((2, SIDE, SIDE), f32),
            pltpu.VMEM((SIDE, SIDE), f32),
            pltpu.VMEM((SIDE, SIDE), f32),
            pltpu.VMEM((N_VERT - 1, SHARE, SIDE), f32),
            pltpu.VMEM((N_VERT - 1, SHARE, SIDE), f32),
            pltpu.VMEM((2 * CPS, 128, 384), bf16),
            dma((5,)),
            dma((2, N_LINE)), dma((2, N_LINE)),
            dma((N_LINE,)), dma((N_LINE,)),
            dma((3, N_LINE)), dma((3, N_LINE)),
            dma((2,)), dma((2,)), dma((2,)), dma((2,)),
            dma((5,)), dma((5,)), dma((3,)), dma((3,)),
        ],
        compiler_params=pltpu.CompilerParams(
            collective_id=0, has_side_effects=True, vmem_limit_bytes=60 * 1024 * 1024
        ),
    )(warped_image, variance, kernel_factors.transpose(1, 0, 2), cell_source, coverage)
    weight_sum = jnp.maximum(weight_sum, 0.5)
    return top_sum / weight_sum, weight_sum


def solution(mesh):
    placed = (
        P("vert", "py", "px"),
        P("vert", "py", "px"),
        P("vert", ("py", "px"), None),
        P("vert", ("py", "px")),
        P("vert", ("py", "px")),
    )
    return jax.shard_map(
        shards,
        mesh=mesh,
        in_specs=placed,
        out_specs=(P(("py", "vert"), "px"), P(("py", "vert"), "px")),
        check_vma=False,
    )
```

```python
import jax
import jax.numpy as jnp
from jax import lax
from jax.experimental import pallas as pl
from jax.experimental.pallas import tpu as pltpu
from jax.sharding import PartitionSpec as P

TAPS = 41
RANK = 3
CELL = 64
HALF = 20
CPS = 6
SIDE = 384
CELLS = 36
PAD = 40
FACT = 246
BORDER = 24
ROWS = SIDE + 2 * BORDER
WINDOW = 80
SHARE = 96
SLICE = 32
LINE = 384
CHUNK = 72
N_VERT = 4
N_LINE = 8
STORE = N_LINE * LINE

MESH = pl.DeviceIdType.MESH
f32 = jnp.float32
bf16 = jnp.bfloat16


def lanes(rows):
    return lax.broadcasted_iota(jnp.int32, (rows, 128), 1)


def turn(x, shift):
    shift = shift % 128
    return x if shift == 0 else pltpu.roll(x, shift, 1)


def split(x):
    high = x.astype(bf16)
    low = (x - high.astype(f32)).astype(bf16)
    return high, low


def kernel(
    img, var_in, fac_in, cs_in, cov_in,
    top_sum, weight_sum,
    ext, var, fac, cs, cov, cells, slices, column, packed, hot, sbuf, rbuf, taps, xs, xr, thi, tlo, weight, num, den,
    rnum, rden, halves,
    in_sem, zsend, zrecv, psend, precv, ssend, srecv, hsend, hrecv, xsend, xrecv,
    nsend, nrecv, dsend, drecv,
):
    a = lax.axis_index("py")
    b = lax.axis_index("px")
    x = lax.axis_index("vert")
    others = (lax.rem(x + 2, N_VERT), N_VERT - 1 - x, x + 1 - 2 * lax.rem(x, 2))

    def at_py(d):
        return {"py": lax.rem(a + d, N_LINE)}

    def at_px(d):
        return {"px": lax.rem(b + d, N_LINE)}

    def remote(src, dst, send, recv, device):
        return pltpu.make_async_remote_copy(
            src_ref=src, dst_ref=dst, send_sem=send, recv_sem=recv,
            device_id=device, device_id_type=MESH,
        )

    barrier = pltpu.get_barrier_semaphore()
    for d in range(1, N_LINE):
        pl.semaphore_signal(barrier, inc=1, device_id=at_py(d), device_id_type=MESH)
    for d in range(1, N_LINE):
        pl.semaphore_signal(barrier, inc=1, device_id=at_px(d), device_id_type=MESH)
    for target in others:
        pl.semaphore_signal(barrier, inc=1, device_id={"vert": target}, device_id_type=MESH)

    inputs = [
        pltpu.make_async_copy(source, target, in_sem.at[n])
        for n, (source, target) in enumerate((
            (fac_in, fac), (cs_in, cs), (cov_in, cov), (var_in, var),
            (img, ext.at[:, pl.ds(BORDER, SIDE), :]),
        ))
    ]
    for copy in inputs:
        copy.start()

    inputs[0].wait()
    cells[...] = jnp.zeros((128, 256), f32)
    for v in range(2):
        cells[CELLS * v:CELLS * (v + 1), 0:FACT] = fac[:, v, :]
    for n in range(2):
        slices[4 * n:4 * (n + 1), 0:SLICE] = cells[:, 128 * n:128 * (n + 1)].T.reshape(4, SLICE, 128)
    inputs[1].wait()
    slices[:, SLICE:SLICE + 8] = jnp.full((N_LINE, 8, 128), -1.0, f32)
    for n in range(N_LINE):
        slices[n, SLICE:SLICE + 2, 0:CELLS] = cs[...].astype(f32)
    column[a] = slices[a]

    pl.semaphore_wait(barrier, 2 * (N_LINE - 1) + N_VERT - 1)

    z_copies = [
        remote(
            slices.at[lax.rem(a + d, N_LINE)], column.at[a], zsend.at[d], zrecv.at[N_LINE - d],
            at_py(d),
        )
        for d in (4, 3, 5, 2, 6, 1, 7)
    ]
    h_down = remote(
        img.at[:, pl.ds(SIDE - BORDER, BORDER), :], ext.at[:, pl.ds(0, BORDER), :],
        hsend.at[0], hrecv.at[0], at_py(1),
    )
    h_up = remote(
        img.at[:, pl.ds(0, BORDER), :], ext.at[:, pl.ds(BORDER + SIDE, BORDER), :],
        hsend.at[1], hrecv.at[1], at_py(N_LINE - 1),
    )
    for copy in z_copies + [h_down, h_up]:
        copy.start()

    inputs[2].wait()
    inputs[3].wait()

    def weight_rows(r, carry):
        rows = pl.ds(pl.multiple_of(r * CELL, CELL), CELL)
        lane = lanes(CELL)
        for c in range(CPS // 2):
            cols = pl.ds(128 * c, 128)
            total = jnp.zeros((CELL, 128), f32)
            for v in range(2):
                left = cov[v, r * CPS + 2 * c].astype(f32)
                right = cov[v, r * CPS + 2 * c + 1].astype(f32)
                w = jnp.where(lane < CELL, left, right) / var[v, rows, cols]
                weight[v, rows, cols] = w
                total = total + w
            den[rows, cols] = total
            num[rows, cols] = jnp.zeros((CELL, 128), f32)
        return carry

    lax.fori_loop(0, CPS, weight_rows, 0)

    def share(ref, t):
        return ref.at[pl.ds(pl.multiple_of(t * SHARE, SHARE), SHARE)]

    den_copies = [
        remote(share(den, t), rden.at[n], dsend.at[n], drecv.at[n], {"vert": t})
        for n, t in enumerate(others)
    ]
    for copy in den_copies:
        copy.start()

    def share_part(n, first, count, sem):
        t = others[n]
        first = first + lax.rem(t, 2) * (SHARE - count - 2 * first)
        first = pl.multiple_of(first, 32)
        base = pl.multiple_of(t * SHARE + first, 32)
        return remote(
            num.at[pl.ds(base, count)], rnum.at[n, pl.ds(first, count)],
            nsend.at[sem], nrecv.at[sem], {"vert": t},
        )

    for copy in z_copies:
        copy.wait_recv()
    lane = lanes(SLICE)

    def gather_tiles(v):
        for t in range(3):
            tile = jnp.zeros((SLICE, 128), f32)
            for i in range(min(3, N_LINE - 3 * t)):
                inside = (lane >= CELLS * i) & (lane < CELLS * (i + 1))
                part = turn(column[3 * t + i, 0:SLICE], CELLS * (i - v))
                tile = jnp.where(inside, part, tile)
            packed[b, v, :, 128 * t:128 * (t + 1)] = tile

    p_copies = [
        [
            remote(
                packed.at[b, v], packed.at[b, v], psend.at[v, d], precv.at[v, N_LINE - d], at_px(d)
            )
            for d in range(1, N_LINE)
        ]
        for v in range(2)
    ]
    gather_tiles(0)
    for copy in p_copies[0]:
        copy.start()

    inputs[4].wait()
    h_down.wait_recv()
    h_up.wait_recv()

    @pl.when(a == 0)
    def _():
        ext[:, 0:BORDER, :] = jnp.zeros((2, BORDER, SIDE), f32)

    @pl.when(a == N_LINE - 1)
    def _():
        ext[:, BORDER + SIDE:ROWS, :] = jnp.zeros((2, BORDER, SIDE), f32)

    def pack(v, carry):
        lane = lanes(CHUNK)
        last = jnp.zeros((CHUNK, 128), f32)
        first = jnp.zeros((CHUNK, 128), f32)
        for g in range(ROWS // CHUNK):
            inside = (lane >= HALF * g) & (lane < HALF * (g + 1))
            rows = slice(CHUNK * g, CHUNK * (g + 1))
            last = jnp.where(inside, turn(ext[v, rows, 256:384], HALF * g - 108), last)
            first = jnp.where(inside, turn(ext[v, rows, 0:128], HALF * g), first)
        xs[0, v] = last
        xs[1, v] = first
        return carry

    lax.fori_loop(0, 2, pack, 0)
    x_copies = [
        remote(xs.at[0], xr.at[0], xsend.at[0], xrecv.at[0], at_px(1)),
        remote(xs.at[1], xr.at[1], xsend.at[1], xrecv.at[1], at_px(N_LINE - 1)),
    ]
    for copy in x_copies:
        copy.start()

    gather_tiles(1)
    for copy in p_copies[1]:
        copy.start()

    names = jnp.concatenate(
        [column[lax.rem(a + d, N_LINE), SLICE:SLICE + 8] for d in range(N_LINE)], axis=0
    )
    wanted = jnp.concatenate([names, names], axis=0).T
    lane = lax.broadcasted_iota(jnp.int32, (1, LINE), 1)
    tile = (lane >= 128).astype(jnp.int32) + (lane >= 256).astype(jnp.int32)
    lane = lane - 128 * tile
    place = (lane >= CELLS).astype(jnp.int32) + (lane >= 2 * CELLS).astype(jnp.int32)
    owner = 3 * tile + place
    stored = owner * (N_LINE * CELLS) + (lane - CELLS * place)
    held = (lane < 3 * CELLS) & (owner < N_LINE)
    stored = jnp.concatenate(
        [jnp.where(held, stored + CELLS * n, -2) for n in range(N_LINE)], axis=1
    ).astype(f32)
    for v in range(2):
        for d in range(0, N_LINE, 2):
            hot[v, PAD * d:PAD * (d + 2)] = jnp.concatenate(
                [
                    jnp.where(wanted[0:PAD, 8 * n + v:8 * n + v + 1] == stored, 1.0, 0.0)
                    for n in (d, d + 1)
                ],
                axis=0,
            ).astype(bf16)

    s_copies = [
        [
            remote(
                sbuf.at[v, d], rbuf.at[v, a], ssend.at[v, d], srecv.at[v, N_LINE - d], at_py(d)
            )
            for d in (4, 3, 5, 2, 6, 1, 7)
        ]
        for v in range(2)
    ]

    def pick(v):
        for copy in p_copies[v]:
            copy.wait_recv()
        high, low = split(jnp.concatenate([packed[n, v] for n in range(N_LINE)], axis=1))
        table = jnp.concatenate([high, low, jnp.zeros((64, STORE), bf16)], axis=0)
        picked = lax.dot_general(
            hot[v], table, (((1,), (1,)), ((), ())), preferred_element_type=f32
        )
        picked = picked + turn(picked, -SLICE)
        groups = picked.reshape(N_LINE, 5, 8, 128)
        groups = [groups[:, g].reshape(8 * N_LINE, 128) for g in range(5)]
        lane = lanes(8 * N_LINE)
        first = groups[0]
        for g in range(1, 4):
            first = jnp.where(lane < SLICE * g, first, turn(groups[g], SLICE * g))
        sbuf[v, :, 0:8] = first.reshape(N_LINE, 8, 128)
        sbuf[v, :, 8:16] = groups[4].reshape(N_LINE, 8, 128)
        rbuf[v, a] = sbuf[v, 0]
        for copy in s_copies[v]:
            copy.start()

    pick(0)

    for copy in x_copies:
        copy.wait_recv()

    def tiles(v):
        tall = 2 * CHUNK
        lane = lanes(tall)
        for j in range(ROWS // tall):
            rows = slice(tall * j, tall * (j + 1))
            raw = [ext[v, rows, 128 * d:128 * (d + 1)] for d in range(3)]
            even = [turn(t, HALF) for t in raw]
            odd = [turn(t, 84) for t in raw]
            border = xr[0, v]
            left = jnp.concatenate(
                [turn(border, -HALF * g) for g in (2 * j, 2 * j + 1)], axis=0
            )
            left = jnp.where(b == 0, 0.0, left)
            border = xr[1, v]
            right = jnp.concatenate(
                [turn(border, 84 - HALF * g) for g in (2 * j, 2 * j + 1)], axis=0
            )
            right = jnp.where(b == N_LINE - 1, 0.0, right)
            before = [left] + even
            after = odd + [right]
            for d in range(3):
                high, low = split(jnp.where(lane < HALF, before[d], even[d]))
                thi[v, 2 * d, rows] = high
                tlo[v, 2 * d, rows] = low
                high, low = split(jnp.where(lane < 84, odd[d], after[d + 1]))
                thi[v, 2 * d + 1, rows] = high
                tlo[v, 2 * d + 1, rows] = low

    tiles(0)
    tiles(1)
    pick(1)

    half = CELL // 2

    def receive_taps(v):
        for copy in s_copies[v]:
            copy.wait_recv()
        lane = lanes(8)
        total = []
        for n in range(2):
            groups = []
            for g in range(5):
                rows, shift = (slice(0, 8), SLICE * g) if g < 4 else (slice(8, 16), 0)
                piece = turn(rbuf[v, 4 * n, rows], -shift)
                for i in range(1, 4):
                    other = turn(rbuf[v, 4 * n + i, rows], SLICE * i - shift)
                    piece = jnp.where(lane < SLICE * i, piece, other)
                groups.append(piece)
            total.append(jnp.concatenate(groups, axis=0))
        lane = lanes(PAD)
        for p in range(2 * RANK):
            n, offset = divmod(TAPS * p, 128)
            tap = turn(total[n], -offset)
            if offset + TAPS > 128:
                rest = turn(total[n + 1], -offset)
                tap = jnp.where(lane < 128 - offset, tap, rest)
            tap = jnp.where(lane < TAPS, tap, 0.0)
            high = tap.astype(bf16).astype(f32)
            taps[v, p, 0] = high
            taps[v, p, 1] = tap - high

    def band(v, p, part, q, count, shift):
        row = jnp.broadcast_to(taps[v, p, part, pl.ds(q, 1), :], (count, 128))
        return pltpu.roll(row, shift, 1, stride=1, stride_axis=0)

    def row_bands(v, q):
        lane = lanes(half)
        parts = []
        for k in range(RANK):
            near = band(v, 2 * k, 0, q, half, 4)
            low = band(v, 2 * k, 1, q, half, WINDOW + 4)
            far = band(v, 2 * k, 0, q, half, 2 * WINDOW + 4 - 128)
            parts.append(
                jnp.concatenate(
                    [
                        jnp.where(lane < WINDOW, near, low),
                        jnp.where(lane < 2 * WINDOW - 128, low, far),
                    ],
                    axis=1,
                )
            )
        return jnp.concatenate(parts, axis=0).astype(bf16)

    def col_bands(v, q):
        return jnp.concatenate(
            [
                jnp.concatenate(
                    [band(v, 2 * k + 1, part, q, CELL, 0) for k in range(RANK)], axis=1
                )
                for part in range(2)
            ],
            axis=0,
        ).astype(bf16)

    def visit_and_row(step):
        late = step // 6
        visit = lax.rem(step // 3, 2)
        place = lax.rem(step, 3)
        flip = lax.rem(x + late, 2)
        place = place + flip * (2 - 2 * place)
        side = x // 2
        return visit, 3 * ((1 - side) * (1 - late) + side * late) + place

    def row_pass(step):
        v, r = visit_and_row(step)
        top = pl.multiple_of(r * CELL, CELL)
        for c in range(CPS):
            windows = []
            for h in range(2):
                rows = pl.ds(pl.multiple_of(top + half * h, half), WINDOW)
                high = thi[v, c, rows, :]
                windows.append(
                    jnp.concatenate([high, high, tlo[v, c, rows, :], high[0:16]], axis=0)
                )
            part = jnp.dot(
                row_bands(v, r * CPS + c), jnp.concatenate(windows, axis=1),
                preferred_element_type=f32,
            )
            halves[lax.rem(step, 2) * CPS + c] = jnp.concatenate(
                [
                    jnp.concatenate(
                        [
                            piece[half * k:half * (k + 1), 128 * h:128 * (h + 1)]
                            for k in range(RANK)
                        ],
                        axis=1,
                    )
                    for piece in split(part)
                    for h in range(2)
                ],
                axis=0,
            )

    def col_pass(step):
        v, r = visit_and_row(step)
        rows = pl.ds(pl.multiple_of(r * CELL, CELL), CELL)
        for c in range(0, CPS, 2):
            pair = []
            for n in (c, c + 1):
                both = lax.dot_general(
                    halves[lax.rem(step, 2) * CPS + n], col_bands(v, r * CPS + n),
                    (((1,), (1,)), ((), ())), preferred_element_type=f32,
                )
                both = both[0:CELL] + both[CELL:2 * CELL]
                pair.append(both + turn(both, CELL))
            cols = slice(CELL * c, CELL * c + 128)
            term = weight[v, rows, cols] * jnp.where(lanes(CELL) < CELL, pair[0], pair[1])
            num[rows, cols] = num[rows, cols] + term

    num_copies = [
        share_part(0, 0, 64, 0), share_part(0, 64, 32, 1), share_part(1, 0, 96, 2),
        share_part(2, 0, 64, 3), share_part(2, 64, 32, 4),
    ]

    receive_taps(0)
    row_pass(jnp.int32(0))

    @pl.loop(1, 3)
    def _(step):
        row_pass(step)
        col_pass(step - 1)

    receive_taps(1)

    @pl.loop(3, 2 * CPS)
    def _(step):
        row_pass(step)
        col_pass(step - 1)
        for copy, ready in zip(num_copies, (4, 5, 6, 10, 11)):

            @pl.when(step == ready)
            def _():
                copy.start()

    col_pass(jnp.int32(2 * CPS - 1))

    mine = pl.ds(pl.multiple_of(x * SHARE, SHARE), SHARE)
    for copy in den_copies + num_copies:
        copy.wait_recv()
    weight_sum[...] = (den[mine] + rden[1]) + (rden[0] + rden[2])
    top_sum[...] = (num[mine] + rnum[1]) + (rnum[0] + rnum[2])

    for copy in z_copies + [h_down, h_up] + x_copies + p_copies[0] + p_copies[1]:
        copy.wait_send()
    for copy in s_copies[0] + s_copies[1] + den_copies + num_copies:
        copy.wait_send()


def shards(warped_image, variance, kernel_factors, cell_source, coverage):
    vmem = pl.BlockSpec(memory_space=pltpu.VMEM)
    dma = pltpu.SemaphoreType.DMA
    out = jax.ShapeDtypeStruct((SHARE, SIDE), f32)
    top_sum, weight_sum = pl.pallas_call(
        kernel,
        out_shape=(out, out),
        in_specs=[pl.BlockSpec(memory_space=pl.ANY)] * 5,
        out_specs=(vmem, vmem),
        scratch_shapes=[
            pltpu.VMEM((2, ROWS, SIDE), f32),
            pltpu.VMEM((2, SIDE, SIDE), f32),
            pltpu.VMEM((CELLS, 2, FACT), f32),
            pltpu.VMEM((2, CELLS), jnp.int32),
            pltpu.SMEM((2, CELLS), jnp.int32),
            pltpu.VMEM((128, 256), f32),
            pltpu.VMEM((N_LINE, SLICE + 8, 128), f32),
            pltpu.VMEM((N_LINE, SLICE + 8, 128), f32),
            pltpu.VMEM((N_LINE, 2, SLICE, LINE), f32),
            pltpu.VMEM((2, N_LINE * PAD, STORE), bf16),
            pltpu.VMEM((2, N_LINE, 16, 128), f32),
            pltpu.VMEM((2, N_LINE, 16, 128), f32),
            pltpu.VMEM((2, 2 * RANK, 2, PAD, 128), f32),
            pltpu.VMEM((2, 2, CHUNK, 128), f32),
            pltpu.VMEM((2, 2, CHUNK, 128), f32),
            pltpu.VMEM((2, CPS, ROWS, 128), bf16),
            pltpu.VMEM((2, CPS, ROWS, 128), bf16),
            pltpu.VMEM((2, SIDE, SIDE), f32),
            pltpu.VMEM((SIDE, SIDE), f32),
            pltpu.VMEM((SIDE, SIDE), f32),
            pltpu.VMEM((N_VERT - 1, SHARE, SIDE), f32),
            pltpu.VMEM((N_VERT - 1, SHARE, SIDE), f32),
            pltpu.VMEM((2 * CPS, 128, 384), bf16),
            dma((5,)),
            dma((N_LINE,)), dma((N_LINE,)),
            dma((2, N_LINE)), dma((2, N_LINE)),
            dma((2, N_LINE)), dma((2, N_LINE)),
            dma((2,)), dma((2,)), dma((2,)), dma((2,)),
            dma((5,)), dma((5,)), dma((3,)), dma((3,)),
        ],
        compiler_params=pltpu.CompilerParams(
            collective_id=0, has_side_effects=True, vmem_limit_bytes=60 * 1024 * 1024
        ),
    )(warped_image, variance, kernel_factors.transpose(1, 0, 2), cell_source, coverage)
    weight_sum = jnp.maximum(weight_sum, 0.5)
    return top_sum / weight_sum, weight_sum


def solution(mesh):
    placed = (
        P("vert", "py", "px"),
        P("vert", "py", "px"),
        P("vert", ("py", "px"), None),
        P("vert", ("py", "px")),
        P("vert", ("py", "px")),
    )
    return jax.shard_map(
        shards,
        mesh=mesh,
        in_specs=placed,
        out_specs=(P(("py", "vert"), "px"), P(("py", "vert"), "px")),
        check_vma=False,
    )
```

```python
import jax
import jax.numpy as jnp
from jax import lax
from jax.experimental import pallas as pl
from jax.experimental.pallas import tpu as pltpu
from jax.sharding import PartitionSpec as P

TAPS = 41
RANK = 3
CELL = 64
HALF = 20
CPS = 6
SIDE = 384
CELLS = 36
PAD = 40
FACT = 246
BORDER = 24
ROWS = SIDE + 2 * BORDER
WINDOW = 80
SHARE = 96
SLICE = 32
LINE = 384
CHUNK = 72
N_VERT = 4
N_LINE = 8
FAR_FIRST = (4, 5, 3, 6, 2, 7, 1)
STORE = N_LINE * LINE

MESH = pl.DeviceIdType.MESH
f32 = jnp.float32
bf16 = jnp.bfloat16


def lanes(rows):
    return lax.broadcasted_iota(jnp.int32, (rows, 128), 1)


def turn(x, shift):
    shift = shift % 128
    return x if shift == 0 else pltpu.roll(x, shift, 1)


def split(x):
    high = x.astype(bf16)
    low = (x - high.astype(f32)).astype(bf16)
    return high, low


def kernel(
    img, var_in, fac_in, cs_in, cov_in,
    top_sum, weight_sum,
    ext, var, fac, cs, cov, cells, slices, column, packed, hot, sbuf, rbuf, taps, xs, xr, thi, tlo, weight, num, den,
    rnum, rden, halves,
    in_sem, zsend, zrecv, psend, precv, ssend, srecv, hsend, hrecv, xsend, xrecv,
    nsend, nrecv, dsend, drecv,
):
    a = lax.axis_index("py")
    b = lax.axis_index("px")
    x = lax.axis_index("vert")
    others = (lax.rem(x + 2, N_VERT), N_VERT - 1 - x, x + 1 - 2 * lax.rem(x, 2))

    def at_py(d):
        return {"py": lax.rem(a + d, N_LINE)}

    def at_px(d):
        return {"px": lax.rem(b + d, N_LINE)}

    def remote(src, dst, send, recv, device):
        return pltpu.make_async_remote_copy(
            src_ref=src, dst_ref=dst, send_sem=send, recv_sem=recv,
            device_id=device, device_id_type=MESH,
        )

    barrier = pltpu.get_barrier_semaphore()
    for d in FAR_FIRST:
        pl.semaphore_signal(barrier, inc=1, device_id=at_py(d), device_id_type=MESH)
    for d in range(1, N_LINE):
        pl.semaphore_signal(barrier, inc=1, device_id=at_px(d), device_id_type=MESH)
    for target in others:
        pl.semaphore_signal(barrier, inc=1, device_id={"vert": target}, device_id_type=MESH)

    inputs = [
        pltpu.make_async_copy(source, target, in_sem.at[n])
        for n, (source, target) in enumerate((
            (fac_in, fac), (cs_in, cs), (cov_in, cov), (var_in, var),
            (img, ext.at[:, pl.ds(BORDER, SIDE), :]),
        ))
    ]
    for copy in inputs:
        copy.start()

    inputs[0].wait()
    cells[...] = jnp.zeros((128, 256), f32)
    for v in range(2):
        cells[CELLS * v:CELLS * (v + 1), 0:FACT] = fac[:, v, :]
    for n in range(2):
        slices[4 * n:4 * (n + 1), 0:SLICE] = cells[:, 128 * n:128 * (n + 1)].T.reshape(4, SLICE, 128)
    inputs[1].wait()
    slices[:, SLICE:SLICE + 8] = jnp.full((N_LINE, 8, 128), -1.0, f32)
    for n in range(N_LINE):
        slices[n, SLICE:SLICE + 2, 0:CELLS] = cs[...].astype(f32)
    column[a] = slices[a]

    pl.semaphore_wait(barrier, 2 * (N_LINE - 1) + N_VERT - 1)

    z_copies = [
        remote(
            slices.at[lax.rem(a + d, N_LINE)], column.at[a], zsend.at[d], zrecv.at[N_LINE - d],
            at_py(d),
        )
        for d in FAR_FIRST
    ]
    h_down = remote(
        img.at[:, pl.ds(SIDE - BORDER, BORDER), :], ext.at[:, pl.ds(0, BORDER), :],
        hsend.at[0], hrecv.at[0], at_py(1),
    )
    h_up = remote(
        img.at[:, pl.ds(0, BORDER), :], ext.at[:, pl.ds(BORDER + SIDE, BORDER), :],
        hsend.at[1], hrecv.at[1], at_py(N_LINE - 1),
    )
    for copy in z_copies + [h_down, h_up]:
        copy.start()

    inputs[2].wait()
    inputs[3].wait()

    def weight_rows(r, carry):
        rows = pl.ds(pl.multiple_of(r * CELL, CELL), CELL)
        lane = lanes(CELL)
        for c in range(CPS // 2):
            cols = pl.ds(128 * c, 128)
            total = jnp.zeros((CELL, 128), f32)
            for v in range(2):
                left = cov[v, r * CPS + 2 * c].astype(f32)
                right = cov[v, r * CPS + 2 * c + 1].astype(f32)
                w = jnp.where(lane < CELL, left, right) / var[v, rows, cols]
                weight[v, rows, cols] = w
                total = total + w
            den[rows, cols] = total
            num[rows, cols] = jnp.zeros((CELL, 128), f32)
        return carry

    lax.fori_loop(0, CPS, weight_rows, 0)

    def share(ref, t):
        return ref.at[pl.ds(pl.multiple_of(t * SHARE, SHARE), SHARE)]

    den_copies = [
        remote(share(den, t), rden.at[n], dsend.at[n], drecv.at[n], {"vert": t})
        for n, t in enumerate(others)
    ]
    for copy in den_copies:
        copy.start()

    def share_part(n, first, count, sem):
        t = others[n]
        first = first + lax.rem(t, 2) * (SHARE - count - 2 * first)
        first = pl.multiple_of(first, 32)
        base = pl.multiple_of(t * SHARE + first, 32)
        return remote(
            num.at[pl.ds(base, count)], rnum.at[n, pl.ds(first, count)],
            nsend.at[sem], nrecv.at[sem], {"vert": t},
        )

    for copy in z_copies:
        copy.wait_recv()
    lane = lanes(SLICE)

    def gather_tiles(v):
        for t in range(3):
            tile = jnp.zeros((SLICE, 128), f32)
            for i in range(min(3, N_LINE - 3 * t)):
                inside = (lane >= CELLS * i) & (lane < CELLS * (i + 1))
                part = turn(column[3 * t + i, 0:SLICE], CELLS * (i - v))
                tile = jnp.where(inside, part, tile)
            packed[b, v, :, 128 * t:128 * (t + 1)] = tile

    p_copies = [
        [
            remote(
                packed.at[b, v], packed.at[b, v], psend.at[v, d], precv.at[v, N_LINE - d], at_px(d)
            )
            for d in FAR_FIRST
        ]
        for v in range(2)
    ]
    gather_tiles(0)
    for copy in p_copies[0]:
        copy.start()

    gather_tiles(1)
    for copy in p_copies[1]:
        copy.start()

    names = jnp.concatenate(
        [column[lax.rem(a + d, N_LINE), SLICE:SLICE + 8] for d in range(N_LINE)], axis=0
    )
    wanted = jnp.concatenate([names, names], axis=0).T
    lane = lax.broadcasted_iota(jnp.int32, (1, LINE), 1)
    tile = (lane >= 128).astype(jnp.int32) + (lane >= 256).astype(jnp.int32)
    lane = lane - 128 * tile
    place = (lane >= CELLS).astype(jnp.int32) + (lane >= 2 * CELLS).astype(jnp.int32)
    owner = 3 * tile + place
    stored = owner * (N_LINE * CELLS) + (lane - CELLS * place)
    held = (lane < 3 * CELLS) & (owner < N_LINE)
    stored = jnp.concatenate(
        [jnp.where(held, stored + CELLS * n, -2) for n in range(N_LINE)], axis=1
    ).astype(f32)
    for v in range(2):
        for d in range(0, N_LINE, 2):
            hot[v, PAD * d:PAD * (d + 2)] = jnp.concatenate(
                [
                    jnp.where(wanted[0:PAD, 8 * n + v:8 * n + v + 1] == stored, 1.0, 0.0)
                    for n in (d, d + 1)
                ],
                axis=0,
            ).astype(bf16)

    inputs[4].wait()
    h_down.wait_recv()
    h_up.wait_recv()

    @pl.when(a == 0)
    def _():
        ext[:, 0:BORDER, :] = jnp.zeros((2, BORDER, SIDE), f32)

    @pl.when(a == N_LINE - 1)
    def _():
        ext[:, BORDER + SIDE:ROWS, :] = jnp.zeros((2, BORDER, SIDE), f32)

    def pack(v, carry):
        lane = lanes(CHUNK)
        last = jnp.zeros((CHUNK, 128), f32)
        first = jnp.zeros((CHUNK, 128), f32)
        for g in range(ROWS // CHUNK):
            inside = (lane >= HALF * g) & (lane < HALF * (g + 1))
            rows = slice(CHUNK * g, CHUNK * (g + 1))
            last = jnp.where(inside, turn(ext[v, rows, 256:384], HALF * g - 108), last)
            first = jnp.where(inside, turn(ext[v, rows, 0:128], HALF * g), first)
        xs[0, v] = last
        xs[1, v] = first
        return carry

    lax.fori_loop(0, 2, pack, 0)
    x_copies = [
        remote(xs.at[0], xr.at[0], xsend.at[0], xrecv.at[0], at_px(1)),
        remote(xs.at[1], xr.at[1], xsend.at[1], xrecv.at[1], at_px(N_LINE - 1)),
    ]
    for copy in x_copies:
        copy.start()

    s_copies = [
        [
            remote(
                sbuf.at[v, d], rbuf.at[v, a], ssend.at[v, d], srecv.at[v, N_LINE - d], at_py(d)
            )
            for d in FAR_FIRST
        ]
        for v in range(2)
    ]

    def pick(v):
        for copy in p_copies[v]:
            copy.wait_recv()
        high, low = split(jnp.concatenate([packed[n, v] for n in range(N_LINE)], axis=1))
        table = jnp.concatenate([high, low, jnp.zeros((64, STORE), bf16)], axis=0)
        picked = lax.dot_general(
            hot[v], table, (((1,), (1,)), ((), ())), preferred_element_type=f32
        )
        picked = picked + turn(picked, -SLICE)
        groups = picked.reshape(N_LINE, 5, 8, 128)
        groups = [groups[:, g].reshape(8 * N_LINE, 128) for g in range(5)]
        lane = lanes(8 * N_LINE)
        first = groups[0]
        for g in range(1, 4):
            first = jnp.where(lane < SLICE * g, first, turn(groups[g], SLICE * g))
        sbuf[v, :, 0:8] = first.reshape(N_LINE, 8, 128)
        sbuf[v, :, 8:16] = groups[4].reshape(N_LINE, 8, 128)
        rbuf[v, a] = sbuf[v, 0]
        for copy in s_copies[v]:
            copy.start()

    pick(0)
    pick(1)

    for copy in x_copies:
        copy.wait_recv()

    def tiles(v):
        tall = 2 * CHUNK
        lane = lanes(tall)
        for j in range(ROWS // tall):
            rows = slice(tall * j, tall * (j + 1))
            raw = [ext[v, rows, 128 * d:128 * (d + 1)] for d in range(3)]
            even = [turn(t, HALF) for t in raw]
            odd = [turn(t, 84) for t in raw]
            border = xr[0, v]
            left = jnp.concatenate(
                [turn(border, -HALF * g) for g in (2 * j, 2 * j + 1)], axis=0
            )
            left = jnp.where(b == 0, 0.0, left)
            border = xr[1, v]
            right = jnp.concatenate(
                [turn(border, 84 - HALF * g) for g in (2 * j, 2 * j + 1)], axis=0
            )
            right = jnp.where(b == N_LINE - 1, 0.0, right)
            before = [left] + even
            after = odd + [right]
            for d in range(3):
                high, low = split(jnp.where(lane < HALF, before[d], even[d]))
                thi[v, 2 * d, rows] = high
                tlo[v, 2 * d, rows] = low
                high, low = split(jnp.where(lane < 84, odd[d], after[d + 1]))
                thi[v, 2 * d + 1, rows] = high
                tlo[v, 2 * d + 1, rows] = low

    tiles(0)
    tiles(1)

    half = CELL // 2

    def receive_taps(v):
        for copy in s_copies[v]:
            copy.wait_recv()
        lane = lanes(8)
        total = []
        for n in range(2):
            groups = []
            for g in range(5):
                rows, shift = (slice(0, 8), SLICE * g) if g < 4 else (slice(8, 16), 0)
                piece = turn(rbuf[v, 4 * n, rows], -shift)
                for i in range(1, 4):
                    other = turn(rbuf[v, 4 * n + i, rows], SLICE * i - shift)
                    piece = jnp.where(lane < SLICE * i, piece, other)
                groups.append(piece)
            total.append(jnp.concatenate(groups, axis=0))
        lane = lanes(PAD)
        for p in range(2 * RANK):
            n, offset = divmod(TAPS * p, 128)
            tap = turn(total[n], -offset)
            if offset + TAPS > 128:
                rest = turn(total[n + 1], -offset)
                tap = jnp.where(lane < 128 - offset, tap, rest)
            tap = jnp.where(lane < TAPS, tap, 0.0)
            high = tap.astype(bf16).astype(f32)
            taps[v, p, 0] = high
            taps[v, p, 1] = tap - high

    def band(v, p, part, q, count, shift):
        row = jnp.broadcast_to(taps[v, p, part, pl.ds(q, 1), :], (count, 128))
        return pltpu.roll(row, shift, 1, stride=1, stride_axis=0)

    def row_bands(v, q):
        lane = lanes(half)
        parts = []
        for k in range(RANK):
            near = band(v, 2 * k, 0, q, half, 4)
            low = band(v, 2 * k, 1, q, half, WINDOW + 4)
            far = band(v, 2 * k, 0, q, half, 2 * WINDOW + 4 - 128)
            parts.append(
                jnp.concatenate(
                    [
                        jnp.where(lane < WINDOW, near, low),
                        jnp.where(lane < 2 * WINDOW - 128, low, far),
                    ],
                    axis=1,
                )
            )
        return jnp.concatenate(parts, axis=0).astype(bf16)

    def col_bands(v, q):
        return jnp.concatenate(
            [
                jnp.concatenate(
                    [band(v, 2 * k + 1, part, q, CELL, 0) for k in range(RANK)], axis=1
                )
                for part in range(2)
            ],
            axis=0,
        ).astype(bf16)

    def visit_and_row(step):
        late = step // 6
        here = step - 6 * late
        visit = (1 - late) * (here // 3) + late * lax.rem(here, 2)
        place = (1 - late) * lax.rem(here, 3) + late * (here // 2)
        flip = lax.rem(x + late, 2)
        place = place + flip * (2 - 2 * place)
        side = x // 2
        return visit, 3 * ((1 - side) * (1 - late) + side * late) + place

    def row_pass(step):
        v, r = visit_and_row(step)
        top = pl.multiple_of(r * CELL, CELL)
        for c in range(CPS):
            windows = []
            for h in range(2):
                rows = pl.ds(pl.multiple_of(top + half * h, half), WINDOW)
                high = thi[v, c, rows, :]
                windows.append(
                    jnp.concatenate([high, high, tlo[v, c, rows, :], high[0:16]], axis=0)
                )
            part = jnp.dot(
                row_bands(v, r * CPS + c), jnp.concatenate(windows, axis=1),
                preferred_element_type=f32,
            )
            halves[lax.rem(step, 2) * CPS + c] = jnp.concatenate(
                [
                    jnp.concatenate(
                        [
                            piece[half * k:half * (k + 1), 128 * h:128 * (h + 1)]
                            for k in range(RANK)
                        ],
                        axis=1,
                    )
                    for piece in split(part)
                    for h in range(2)
                ],
                axis=0,
            )

    def col_pass(step):
        v, r = visit_and_row(step)
        rows = pl.ds(pl.multiple_of(r * CELL, CELL), CELL)
        for c in range(0, CPS, 2):
            pair = []
            for n in (c, c + 1):
                both = lax.dot_general(
                    halves[lax.rem(step, 2) * CPS + n], col_bands(v, r * CPS + n),
                    (((1,), (1,)), ((), ())), preferred_element_type=f32,
                )
                both = both[0:CELL] + both[CELL:2 * CELL]
                pair.append(both + turn(both, CELL))
            cols = slice(CELL * c, CELL * c + 128)
            term = weight[v, rows, cols] * jnp.where(lanes(CELL) < CELL, pair[0], pair[1])
            num[rows, cols] = num[rows, cols] + term

    num_copies = [
        share_part(0, 0, 64, 0), share_part(0, 64, 32, 1), share_part(1, 0, 96, 2),
        share_part(2, 0, 64, 3), share_part(2, 64, 32, 4),
    ]

    receive_taps(0)
    row_pass(jnp.int32(0))

    @pl.loop(1, 3)
    def _(step):
        row_pass(step)
        col_pass(step - 1)

    receive_taps(1)

    @pl.loop(3, 2 * CPS)
    def _(step):
        row_pass(step)
        col_pass(step - 1)
        for copy, ready in zip(num_copies, (4, 5, 6, 8, 10)):

            @pl.when(step == ready)
            def _():
                copy.start()

    col_pass(jnp.int32(2 * CPS - 1))

    mine = pl.ds(pl.multiple_of(x * SHARE, SHARE), SHARE)
    for copy in den_copies + num_copies:
        copy.wait_recv()
    weight_sum[...] = (den[mine] + rden[1]) + (rden[0] + rden[2])
    top_sum[...] = (num[mine] + rnum[1]) + (rnum[0] + rnum[2])

    for copy in z_copies + [h_down, h_up] + x_copies + p_copies[0] + p_copies[1]:
        copy.wait_send()
    for copy in s_copies[0] + s_copies[1] + den_copies + num_copies:
        copy.wait_send()


def shards(warped_image, variance, kernel_factors, cell_source, coverage):
    vmem = pl.BlockSpec(memory_space=pltpu.VMEM)
    dma = pltpu.SemaphoreType.DMA
    out = jax.ShapeDtypeStruct((SHARE, SIDE), f32)
    top_sum, weight_sum = pl.pallas_call(
        kernel,
        out_shape=(out, out),
        in_specs=[pl.BlockSpec(memory_space=pl.ANY)] * 5,
        out_specs=(vmem, vmem),
        scratch_shapes=[
            pltpu.VMEM((2, ROWS, SIDE), f32),
            pltpu.VMEM((2, SIDE, SIDE), f32),
            pltpu.VMEM((CELLS, 2, FACT), f32),
            pltpu.VMEM((2, CELLS), jnp.int32),
            pltpu.SMEM((2, CELLS), jnp.int32),
            pltpu.VMEM((128, 256), f32),
            pltpu.VMEM((N_LINE, SLICE + 8, 128), f32),
            pltpu.VMEM((N_LINE, SLICE + 8, 128), f32),
            pltpu.VMEM((N_LINE, 2, SLICE, LINE), f32),
            pltpu.VMEM((2, N_LINE * PAD, STORE), bf16),
            pltpu.VMEM((2, N_LINE, 16, 128), f32),
            pltpu.VMEM((2, N_LINE, 16, 128), f32),
            pltpu.VMEM((2, 2 * RANK, 2, PAD, 128), f32),
            pltpu.VMEM((2, 2, CHUNK, 128), f32),
            pltpu.VMEM((2, 2, CHUNK, 128), f32),
            pltpu.VMEM((2, CPS, ROWS, 128), bf16),
            pltpu.VMEM((2, CPS, ROWS, 128), bf16),
            pltpu.VMEM((2, SIDE, SIDE), f32),
            pltpu.VMEM((SIDE, SIDE), f32),
            pltpu.VMEM((SIDE, SIDE), f32),
            pltpu.VMEM((N_VERT - 1, SHARE, SIDE), f32),
            pltpu.VMEM((N_VERT - 1, SHARE, SIDE), f32),
            pltpu.VMEM((2 * CPS, 128, 384), bf16),
            dma((5,)),
            dma((N_LINE,)), dma((N_LINE,)),
            dma((2, N_LINE)), dma((2, N_LINE)),
            dma((2, N_LINE)), dma((2, N_LINE)),
            dma((2,)), dma((2,)), dma((2,)), dma((2,)),
            dma((5,)), dma((5,)), dma((3,)), dma((3,)),
        ],
        compiler_params=pltpu.CompilerParams(
            collective_id=0, has_side_effects=True, vmem_limit_bytes=60 * 1024 * 1024
        ),
    )(warped_image, variance, kernel_factors.transpose(1, 0, 2), cell_source, coverage)
    weight_sum = jnp.maximum(weight_sum, 0.5)
    return top_sum / weight_sum, weight_sum


def solution(mesh):
    placed = (
        P("vert", "py", "px"),
        P("vert", "py", "px"),
        P("vert", ("py", "px"), None),
        P("vert", ("py", "px")),
        P("vert", ("py", "px")),
    )
    return jax.shard_map(
        shards,
        mesh=mesh,
        in_specs=placed,
        out_specs=(P(("py", "vert"), "px"), P(("py", "vert"), "px")),
        check_vma=False,
    )
```

```python
import jax
import jax.numpy as jnp
from jax import lax
from jax.experimental import pallas as pl
from jax.experimental.pallas import tpu as pltpu
from jax.sharding import PartitionSpec as P

TAPS = 41
RANK = 3
CELL = 64
HALF = 20
CPS = 6
SIDE = 384
CELLS = 36
PAD = 40
FACT = 246
BORDER = 24
ROWS = SIDE + 2 * BORDER
WINDOW = 80
SHARE = 96
EACH = 4
SLICE = 32
LINE = 384
CHUNK = 72
N_VERT = 4
N_LINE = 8
FAR_FIRST = (4, 5, 3, 6, 2, 7, 1)
STORE = N_LINE * LINE

MESH = pl.DeviceIdType.MESH
f32 = jnp.float32
bf16 = jnp.bfloat16


def lanes(rows):
    return lax.broadcasted_iota(jnp.int32, (rows, 128), 1)


def turn(x, shift):
    shift = shift % 128
    return x if shift == 0 else pltpu.roll(x, shift, 1)


def split(x):
    high = x.astype(bf16)
    low = (x - high.astype(f32)).astype(bf16)
    return high, low


def kernel(
    img, var_in, fac_in, cs_in, cov_in,
    top_sum, weight_sum,
    ext, var, fac, cs, cov, cells, slices, column, packed, hot, sbuf, rbuf, taps, xs, xr, thi, tlo, weight, num, den,
    rnum, rden, halves,
    in_sem, zsend, zrecv, psend, precv, ssend, srecv, hsend, hrecv, xsend, xrecv,
    nsend, nrecv, dsend, drecv,
):
    a = lax.axis_index("py")
    b = lax.axis_index("px")
    x = lax.axis_index("vert")
    others = (lax.rem(x + 2, N_VERT), N_VERT - 1 - x, x + 1 - 2 * lax.rem(x, 2))

    def at_py(d):
        return {"py": lax.rem(a + d, N_LINE)}

    def at_px(d):
        return {"px": lax.rem(b + d, N_LINE)}

    def remote(src, dst, send, recv, device):
        return pltpu.make_async_remote_copy(
            src_ref=src, dst_ref=dst, send_sem=send, recv_sem=recv,
            device_id=device, device_id_type=MESH,
        )

    barrier = pltpu.get_barrier_semaphore()
    for d in FAR_FIRST:
        pl.semaphore_signal(barrier, inc=1, device_id=at_py(d), device_id_type=MESH)
    for d in range(1, N_LINE):
        pl.semaphore_signal(barrier, inc=1, device_id=at_px(d), device_id_type=MESH)
    for target in others:
        pl.semaphore_signal(barrier, inc=1, device_id={"vert": target}, device_id_type=MESH)

    inputs = [
        pltpu.make_async_copy(source, target, in_sem.at[n])
        for n, (source, target) in enumerate((
            (fac_in, fac), (cs_in, cs), (cov_in, cov), (var_in, var),
            (img, ext.at[:, pl.ds(BORDER, SIDE), :]),
        ))
    ]
    for copy in inputs:
        copy.start()

    inputs[0].wait()
    cells[...] = jnp.zeros((128, 256), f32)
    for v in range(2):
        cells[CELLS * v:CELLS * (v + 1), 0:FACT] = fac[:, v, :]
    for n in range(2):
        slices[4 * n:4 * (n + 1), 0:SLICE] = cells[:, 128 * n:128 * (n + 1)].T.reshape(4, SLICE, 128)
    inputs[1].wait()
    slices[:, SLICE:SLICE + 8] = jnp.full((N_LINE, 8, 128), -1.0, f32)
    for n in range(N_LINE):
        slices[n, SLICE:SLICE + 2, 0:CELLS] = cs[...].astype(f32)
    column[a] = slices[a]

    pl.semaphore_wait(barrier, 2 * (N_LINE - 1) + N_VERT - 1)

    z_copies = [
        remote(
            slices.at[lax.rem(a + d, N_LINE)], column.at[a], zsend.at[d], zrecv.at[N_LINE - d],
            at_py(d),
        )
        for d in FAR_FIRST
    ]
    h_down = remote(
        img.at[:, pl.ds(SIDE - BORDER, BORDER), :], ext.at[:, pl.ds(0, BORDER), :],
        hsend.at[0], hrecv.at[0], at_py(1),
    )
    h_up = remote(
        img.at[:, pl.ds(0, BORDER), :], ext.at[:, pl.ds(BORDER + SIDE, BORDER), :],
        hsend.at[1], hrecv.at[1], at_py(N_LINE - 1),
    )
    for copy in z_copies + [h_down, h_up]:
        copy.start()

    inputs[2].wait()
    inputs[3].wait()

    def weight_rows(r, carry):
        rows = pl.ds(pl.multiple_of(r * CELL, CELL), CELL)
        lane = lanes(CELL)
        for c in range(CPS // 2):
            cols = pl.ds(128 * c, 128)
            total = jnp.zeros((CELL, 128), f32)
            for v in range(2):
                left = cov[v, r * CPS + 2 * c].astype(f32)
                right = cov[v, r * CPS + 2 * c + 1].astype(f32)
                w = jnp.where(lane < CELL, left, right) / var[v, rows, cols]
                weight[v, rows, cols] = w
                total = total + w
            den[rows, cols] = total
            num[rows, cols] = jnp.zeros((CELL, 128), f32)
        return carry

    lax.fori_loop(0, CPS, weight_rows, 0)

    def share(ref, t):
        return ref.at[pl.ds(pl.multiple_of(t * SHARE, SHARE), SHARE)]

    den_copies = [
        remote(share(den, t), rden.at[n], dsend.at[n], drecv.at[n], {"vert": t})
        for n, t in enumerate(others)
    ]
    for copy in den_copies:
        copy.start()

    def share_part(n, first, count, sem):
        t = others[n]
        first = first + lax.rem(t, 2) * (SHARE - count - 2 * first)
        first = pl.multiple_of(first, 32)
        base = pl.multiple_of(t * SHARE + first, 32)
        return remote(
            num.at[pl.ds(base, count)], rnum.at[n, pl.ds(first, count)],
            nsend.at[sem], nrecv.at[sem], {"vert": t},
        )

    for copy in z_copies:
        copy.wait_recv()
    lane = lanes(SLICE)

    def gather_tiles(v):
        for t in range(3):
            tile = jnp.zeros((SLICE, 128), f32)
            for i in range(min(3, N_LINE - 3 * t)):
                inside = (lane >= CELLS * i) & (lane < CELLS * (i + 1))
                part = turn(column[3 * t + i, 0:SLICE], CELLS * (i - v))
                tile = jnp.where(inside, part, tile)
            packed[b, v, :, 128 * t:128 * (t + 1)] = tile

    p_copies = [
        [
            remote(
                packed.at[b, v], packed.at[b, v], psend.at[v, d], precv.at[v, N_LINE - d], at_px(d)
            )
            for d in FAR_FIRST
        ]
        for v in range(2)
    ]
    gather_tiles(0)
    for copy in p_copies[0]:
        copy.start()

    gather_tiles(1)
    for copy in p_copies[1]:
        copy.start()

    names = jnp.concatenate(
        [column[lax.rem(a + d, N_LINE), SLICE:SLICE + 8] for d in range(N_LINE)], axis=0
    )
    wanted = jnp.concatenate([names, names], axis=0).T
    lane = lax.broadcasted_iota(jnp.int32, (1, LINE), 1)
    tile = (lane >= 128).astype(jnp.int32) + (lane >= 256).astype(jnp.int32)
    lane = lane - 128 * tile
    place = (lane >= CELLS).astype(jnp.int32) + (lane >= 2 * CELLS).astype(jnp.int32)
    owner = 3 * tile + place
    stored = owner * (N_LINE * CELLS) + (lane - CELLS * place)
    held = (lane < 3 * CELLS) & (owner < N_LINE)
    stored = jnp.concatenate(
        [jnp.where(held, stored + CELLS * n, -2) for n in range(N_LINE)], axis=1
    ).astype(f32)
    for v in range(2):
        for d in range(0, N_LINE, 2):
            hot[v, PAD * d:PAD * (d + 2)] = jnp.concatenate(
                [
                    jnp.where(wanted[0:PAD, 8 * n + v:8 * n + v + 1] == stored, 1.0, 0.0)
                    for n in (d, d + 1)
                ],
                axis=0,
            ).astype(bf16)

    inputs[4].wait()
    h_down.wait_recv()
    h_up.wait_recv()

    @pl.when(a == 0)
    def _():
        ext[:, 0:BORDER, :] = jnp.zeros((2, BORDER, SIDE), f32)

    @pl.when(a == N_LINE - 1)
    def _():
        ext[:, BORDER + SIDE:ROWS, :] = jnp.zeros((2, BORDER, SIDE), f32)

    def pack(v, carry):
        lane = lanes(CHUNK)
        last = jnp.zeros((CHUNK, 128), f32)
        first = jnp.zeros((CHUNK, 128), f32)
        for g in range(ROWS // CHUNK):
            inside = (lane >= HALF * g) & (lane < HALF * (g + 1))
            rows = slice(CHUNK * g, CHUNK * (g + 1))
            last = jnp.where(inside, turn(ext[v, rows, 256:384], HALF * g - 108), last)
            first = jnp.where(inside, turn(ext[v, rows, 0:128], HALF * g), first)
        xs[0, v] = last
        xs[1, v] = first
        return carry

    lax.fori_loop(0, 2, pack, 0)
    x_copies = [
        remote(xs.at[0], xr.at[0], xsend.at[0], xrecv.at[0], at_px(1)),
        remote(xs.at[1], xr.at[1], xsend.at[1], xrecv.at[1], at_px(N_LINE - 1)),
    ]
    for copy in x_copies:
        copy.start()

    s_copies = [
        [
            remote(
                sbuf.at[v, d], rbuf.at[v, a], ssend.at[v, d], srecv.at[v, N_LINE - d], at_py(d)
            )
            for d in FAR_FIRST
        ]
        for v in range(2)
    ]

    def pick(v):
        for copy in p_copies[v]:
            copy.wait_recv()
        high, low = split(jnp.concatenate([packed[n, v] for n in range(N_LINE)], axis=1))
        table = jnp.concatenate([high, low, jnp.zeros((64, STORE), bf16)], axis=0)
        picked = lax.dot_general(
            hot[v], table, (((1,), (1,)), ((), ())), preferred_element_type=f32
        )
        picked = picked + turn(picked, -SLICE)
        groups = picked.reshape(N_LINE, 5, 8, 128)
        groups = [groups[:, g].reshape(8 * N_LINE, 128) for g in range(5)]
        lane = lanes(8 * N_LINE)
        first = groups[0]
        for g in range(1, 4):
            first = jnp.where(lane < SLICE * g, first, turn(groups[g], SLICE * g))
        sbuf[v, :, 0:8] = first.reshape(N_LINE, 8, 128)
        sbuf[v, :, 8:16] = groups[4].reshape(N_LINE, 8, 128)
        rbuf[v, a] = sbuf[v, 0]
        for copy in s_copies[v]:
            copy.start()

    pick(0)
    pick(1)

    for copy in x_copies:
        copy.wait_recv()

    def tiles(v):
        tall = 2 * CHUNK
        lane = lanes(tall)
        for j in range(ROWS // tall):
            rows = slice(tall * j, tall * (j + 1))
            raw = [ext[v, rows, 128 * d:128 * (d + 1)] for d in range(3)]
            even = [turn(t, HALF) for t in raw]
            odd = [turn(t, 84) for t in raw]
            border = xr[0, v]
            left = jnp.concatenate(
                [turn(border, -HALF * g) for g in (2 * j, 2 * j + 1)], axis=0
            )
            left = jnp.where(b == 0, 0.0, left)
            border = xr[1, v]
            right = jnp.concatenate(
                [turn(border, 84 - HALF * g) for g in (2 * j, 2 * j + 1)], axis=0
            )
            right = jnp.where(b == N_LINE - 1, 0.0, right)
            before = [left] + even
            after = odd + [right]
            for d in range(3):
                high, low = split(jnp.where(lane < HALF, before[d], even[d]))
                thi[v, 2 * d, rows] = high
                tlo[v, 2 * d, rows] = low
                high, low = split(jnp.where(lane < 84, odd[d], after[d + 1]))
                thi[v, 2 * d + 1, rows] = high
                tlo[v, 2 * d + 1, rows] = low

    tiles(0)
    tiles(1)

    half = CELL // 2

    def receive_taps(v):
        for copy in s_copies[v]:
            copy.wait_recv()
        lane = lanes(8)
        total = []
        for n in range(2):
            groups = []
            for g in range(5):
                rows, shift = (slice(0, 8), SLICE * g) if g < 4 else (slice(8, 16), 0)
                piece = turn(rbuf[v, 4 * n, rows], -shift)
                for i in range(1, 4):
                    other = turn(rbuf[v, 4 * n + i, rows], SLICE * i - shift)
                    piece = jnp.where(lane < SLICE * i, piece, other)
                groups.append(piece)
            total.append(jnp.concatenate(groups, axis=0))
        lane = lanes(PAD)
        for p in range(2 * RANK):
            n, offset = divmod(TAPS * p, 128)
            tap = turn(total[n], -offset)
            if offset + TAPS > 128:
                rest = turn(total[n + 1], -offset)
                tap = jnp.where(lane < 128 - offset, tap, rest)
            tap = jnp.where(lane < TAPS, tap, 0.0)
            high = tap.astype(bf16).astype(f32)
            taps[v, p, 0] = high
            taps[v, p, 1] = tap - high

    def band(v, p, part, q, count, shift):
        row = jnp.broadcast_to(taps[v, p, part, pl.ds(q, 1), :], (count, 128))
        return pltpu.roll(row, shift, 1, stride=1, stride_axis=0)

    def row_bands(v, q):
        lane = lanes(half)
        parts = []
        for k in range(RANK):
            near = band(v, 2 * k, 0, q, half, 4)
            low = band(v, 2 * k, 1, q, half, WINDOW + 4)
            far = band(v, 2 * k, 0, q, half, 2 * WINDOW + 4 - 128)
            parts.append(
                jnp.concatenate(
                    [
                        jnp.where(lane < WINDOW, near, low),
                        jnp.where(lane < 2 * WINDOW - 128, low, far),
                    ],
                    axis=1,
                )
            )
        return jnp.concatenate(parts, axis=0).astype(bf16)

    def col_bands(v, q):
        return jnp.concatenate(
            [
                jnp.concatenate(
                    [band(v, 2 * k + 1, part, q, CELL, 0) for k in range(RANK)], axis=1
                )
                for part in range(2)
            ],
            axis=0,
        ).astype(bf16)

    def visit_and_row(step):
        late = step // (2 * EACH)
        visit = (1 - late) * (step // EACH) + late * lax.rem(step, 2)
        place = (1 - late) * lax.rem(step, EACH) + late * (step // 2)
        near = place // 3
        place = place - 3 * near
        flip = lax.rem(x + near, 2)
        place = place + flip * (2 - 2 * place)
        side = x // 2
        return visit, 3 * ((1 - side) * (1 - near) + side * near) + place

    def row_pass(step):
        v, r = visit_and_row(step)
        top = pl.multiple_of(r * CELL, CELL)
        for c in range(CPS):
            windows = []
            for h in range(2):
                rows = pl.ds(pl.multiple_of(top + half * h, half), WINDOW)
                high = thi[v, c, rows, :]
                windows.append(
                    jnp.concatenate([high, high, tlo[v, c, rows, :], high[0:16]], axis=0)
                )
            part = jnp.dot(
                row_bands(v, r * CPS + c), jnp.concatenate(windows, axis=1),
                preferred_element_type=f32,
            )
            halves[lax.rem(step, 2) * CPS + c] = jnp.concatenate(
                [
                    jnp.concatenate(
                        [
                            piece[half * k:half * (k + 1), 128 * h:128 * (h + 1)]
                            for k in range(RANK)
                        ],
                        axis=1,
                    )
                    for piece in split(part)
                    for h in range(2)
                ],
                axis=0,
            )

    def col_pass(step):
        v, r = visit_and_row(step)
        rows = pl.ds(pl.multiple_of(r * CELL, CELL), CELL)
        for c in range(0, CPS, 2):
            pair = []
            for n in (c, c + 1):
                both = lax.dot_general(
                    halves[lax.rem(step, 2) * CPS + n], col_bands(v, r * CPS + n),
                    (((1,), (1,)), ((), ())), preferred_element_type=f32,
                )
                both = both[0:CELL] + both[CELL:2 * CELL]
                pair.append(both + turn(both, CELL))
            cols = slice(CELL * c, CELL * c + 128)
            term = weight[v, rows, cols] * jnp.where(lanes(CELL) < CELL, pair[0], pair[1])
            num[rows, cols] = num[rows, cols] + term

    num_copies = [
        share_part(0, 0, 64, 0), share_part(0, 64, 32, 1), share_part(1, 0, 96, 2),
        share_part(2, 0, 64, 3), share_part(2, 64, 32, 4),
    ]

    receive_taps(0)
    row_pass(jnp.int32(0))

    @pl.loop(1, EACH)
    def _(step):
        row_pass(step)
        col_pass(step - 1)

    receive_taps(1)

    @pl.loop(EACH, 2 * CPS)
    def _(step):
        row_pass(step)
        col_pass(step - 1)
        for copy, ready in zip(num_copies, (5, 6, 7, 8, 10)):

            @pl.when(step == ready)
            def _():
                copy.start()

    col_pass(jnp.int32(2 * CPS - 1))

    mine = pl.ds(pl.multiple_of(x * SHARE, SHARE), SHARE)
    for copy in den_copies + num_copies:
        copy.wait_recv()
    weight_sum[...] = (den[mine] + rden[1]) + (rden[0] + rden[2])
    top_sum[...] = (num[mine] + rnum[1]) + (rnum[0] + rnum[2])

    for copy in z_copies + [h_down, h_up] + x_copies + p_copies[0] + p_copies[1]:
        copy.wait_send()
    for copy in s_copies[0] + s_copies[1] + den_copies + num_copies:
        copy.wait_send()


def shards(warped_image, variance, kernel_factors, cell_source, coverage):
    vmem = pl.BlockSpec(memory_space=pltpu.VMEM)
    dma = pltpu.SemaphoreType.DMA
    out = jax.ShapeDtypeStruct((SHARE, SIDE), f32)
    top_sum, weight_sum = pl.pallas_call(
        kernel,
        out_shape=(out, out),
        in_specs=[pl.BlockSpec(memory_space=pl.ANY)] * 5,
        out_specs=(vmem, vmem),
        scratch_shapes=[
            pltpu.VMEM((2, ROWS, SIDE), f32),
            pltpu.VMEM((2, SIDE, SIDE), f32),
            pltpu.VMEM((CELLS, 2, FACT), f32),
            pltpu.VMEM((2, CELLS), jnp.int32),
            pltpu.SMEM((2, CELLS), jnp.int32),
            pltpu.VMEM((128, 256), f32),
            pltpu.VMEM((N_LINE, SLICE + 8, 128), f32),
            pltpu.VMEM((N_LINE, SLICE + 8, 128), f32),
            pltpu.VMEM((N_LINE, 2, SLICE, LINE), f32),
            pltpu.VMEM((2, N_LINE * PAD, STORE), bf16),
            pltpu.VMEM((2, N_LINE, 16, 128), f32),
            pltpu.VMEM((2, N_LINE, 16, 128), f32),
            pltpu.VMEM((2, 2 * RANK, 2, PAD, 128), f32),
            pltpu.VMEM((2, 2, CHUNK, 128), f32),
            pltpu.VMEM((2, 2, CHUNK, 128), f32),
            pltpu.VMEM((2, CPS, ROWS, 128), bf16),
            pltpu.VMEM((2, CPS, ROWS, 128), bf16),
            pltpu.VMEM((2, SIDE, SIDE), f32),
            pltpu.VMEM((SIDE, SIDE), f32),
            pltpu.VMEM((SIDE, SIDE), f32),
            pltpu.VMEM((N_VERT - 1, SHARE, SIDE), f32),
            pltpu.VMEM((N_VERT - 1, SHARE, SIDE), f32),
            pltpu.VMEM((2 * CPS, 128, 384), bf16),
            dma((5,)),
            dma((N_LINE,)), dma((N_LINE,)),
            dma((2, N_LINE)), dma((2, N_LINE)),
            dma((2, N_LINE)), dma((2, N_LINE)),
            dma((2,)), dma((2,)), dma((2,)), dma((2,)),
            dma((5,)), dma((5,)), dma((3,)), dma((3,)),
        ],
        compiler_params=pltpu.CompilerParams(
            collective_id=0, has_side_effects=True, vmem_limit_bytes=60 * 1024 * 1024
        ),
    )(warped_image, variance, kernel_factors.transpose(1, 0, 2), cell_source, coverage)
    weight_sum = jnp.maximum(weight_sum, 0.5)
    return top_sum / weight_sum, weight_sum


def solution(mesh):
    placed = (
        P("vert", "py", "px"),
        P("vert", "py", "px"),
        P("vert", ("py", "px"), None),
        P("vert", ("py", "px")),
        P("vert", ("py", "px")),
    )
    return jax.shard_map(
        shards,
        mesh=mesh,
        in_specs=placed,
        out_specs=(P(("py", "vert"), "px"), P(("py", "vert"), "px")),
        check_vma=False,
    )
```

```python
import jax
import jax.numpy as jnp
from jax import lax
from jax.experimental import pallas as pl
from jax.experimental.pallas import tpu as pltpu
from jax.sharding import PartitionSpec as P

TAPS = 41
RANK = 3
CELL = 64
HALF = 20
CPS = 6
SIDE = 384
CELLS = 36
PAD = 40
FACT = 246
BORDER = 24
ROWS = SIDE + 2 * BORDER
WINDOW = 80
SHARE = 96
EACH = 4
SLICE = 32
LINE = 384
CHUNK = 72
N_VERT = 4
N_LINE = 8
FAR_FIRST = (4, 5, 3, 6, 2, 7, 1)
STORE = N_LINE * LINE

MESH = pl.DeviceIdType.MESH
f32 = jnp.float32
bf16 = jnp.bfloat16


def lanes(rows):
    return lax.broadcasted_iota(jnp.int32, (rows, 128), 1)


def turn(x, shift):
    shift = shift % 128
    return x if shift == 0 else pltpu.roll(x, shift, 1)


def split(x):
    high = x.astype(bf16)
    low = (x - high.astype(f32)).astype(bf16)
    return high, low


def kernel(
    img, var_in, fac_in, cs_in, cov_in,
    top_sum, weight_sum,
    ext, var, fac, cs, cov, cells, slices, column, packed, hot, sbuf, rbuf, taps, xs, xr, thi, tlo, weight, num, den,
    rnum, rden, halves,
    in_sem, zsend, zrecv, psend, precv, ssend, srecv, hsend, hrecv, xsend, xrecv,
    nsend, nrecv, dsend, drecv,
):
    a = lax.axis_index("py")
    b = lax.axis_index("px")
    x = lax.axis_index("vert")
    others = (lax.rem(x + 2, N_VERT), N_VERT - 1 - x, x + 1 - 2 * lax.rem(x, 2))

    def at_py(d):
        return {"py": lax.rem(a + d, N_LINE)}

    def at_px(d):
        return {"px": lax.rem(b + d, N_LINE)}

    def remote(src, dst, send, recv, device):
        return pltpu.make_async_remote_copy(
            src_ref=src, dst_ref=dst, send_sem=send, recv_sem=recv,
            device_id=device, device_id_type=MESH,
        )

    barrier = pltpu.get_barrier_semaphore()
    for d in FAR_FIRST:
        pl.semaphore_signal(barrier, inc=1, device_id=at_py(d), device_id_type=MESH)
    for d in range(1, N_LINE):
        pl.semaphore_signal(barrier, inc=1, device_id=at_px(d), device_id_type=MESH)
    for target in others:
        pl.semaphore_signal(barrier, inc=1, device_id={"vert": target}, device_id_type=MESH)

    inputs = [
        pltpu.make_async_copy(source, target, in_sem.at[n])
        for n, (source, target) in enumerate((
            (fac_in, fac), (cs_in, cs), (cov_in, cov), (var_in, var),
            (img, ext.at[:, pl.ds(BORDER, SIDE), :]),
        ))
    ]
    for copy in inputs:
        copy.start()

    inputs[0].wait()
    cells[...] = jnp.zeros((128, 256), f32)
    for v in range(2):
        cells[CELLS * v:CELLS * (v + 1), 0:FACT] = fac[:, v, :]
    for n in range(2):
        slices[4 * n:4 * (n + 1), 0:SLICE] = cells[:, 128 * n:128 * (n + 1)].T.reshape(4, SLICE, 128)
    inputs[1].wait()
    slices[:, SLICE:SLICE + 8] = jnp.full((N_LINE, 8, 128), -1.0, f32)
    for n in range(N_LINE):
        slices[n, SLICE:SLICE + 2, 0:CELLS] = cs[...].astype(f32)
    column[a] = slices[a]

    pl.semaphore_wait(barrier, 2 * (N_LINE - 1) + N_VERT - 1)

    z_copies = [
        remote(
            slices.at[lax.rem(a + d, N_LINE)], column.at[a], zsend.at[d], zrecv.at[N_LINE - d],
            at_py(d),
        )
        for d in FAR_FIRST
    ]
    h_down = remote(
        img.at[:, pl.ds(SIDE - BORDER, BORDER), :], ext.at[:, pl.ds(0, BORDER), :],
        hsend.at[0], hrecv.at[0], at_py(1),
    )
    h_up = remote(
        img.at[:, pl.ds(0, BORDER), :], ext.at[:, pl.ds(BORDER + SIDE, BORDER), :],
        hsend.at[1], hrecv.at[1], at_py(N_LINE - 1),
    )
    for copy in z_copies + [h_down, h_up]:
        copy.start()

    inputs[2].wait()
    inputs[3].wait()

    def weight_rows(r, carry):
        rows = pl.ds(pl.multiple_of(r * CELL, CELL), CELL)
        lane = lanes(CELL)
        for c in range(CPS // 2):
            cols = pl.ds(128 * c, 128)
            total = jnp.zeros((CELL, 128), f32)
            for v in range(2):
                left = cov[v, r * CPS + 2 * c].astype(f32)
                right = cov[v, r * CPS + 2 * c + 1].astype(f32)
                w = jnp.where(lane < CELL, left, right) / var[v, rows, cols]
                weight[v, rows, cols] = w
                total = total + w
            den[rows, cols] = total
            num[rows, cols] = jnp.zeros((CELL, 128), f32)
        return carry

    lax.fori_loop(0, CPS, weight_rows, 0)

    def share(ref, t):
        return ref.at[pl.ds(pl.multiple_of(t * SHARE, SHARE), SHARE)]

    den_copies = [
        remote(share(den, t), rden.at[n], dsend.at[n], drecv.at[n], {"vert": t})
        for n, t in enumerate(others)
    ]
    for copy in den_copies:
        copy.start()

    def share_part(n, first, count, sem):
        t = others[n]
        first = first + lax.rem(t, 2) * (SHARE - count - 2 * first)
        first = pl.multiple_of(first, 32)
        base = pl.multiple_of(t * SHARE + first, 32)
        return remote(
            num.at[pl.ds(base, count)], rnum.at[n, pl.ds(first, count)],
            nsend.at[sem], nrecv.at[sem], {"vert": t},
        )

    for copy in z_copies:
        copy.wait_recv()
    lane = lanes(SLICE)

    def gather_tiles(v):
        for t in range(3):
            tile = jnp.zeros((SLICE, 128), f32)
            for i in range(min(3, N_LINE - 3 * t)):
                inside = (lane >= CELLS * i) & (lane < CELLS * (i + 1))
                part = turn(column[3 * t + i, 0:SLICE], CELLS * (i - v))
                tile = jnp.where(inside, part, tile)
            packed[b, v, :, 128 * t:128 * (t + 1)] = tile

    p_copies = [
        [
            remote(
                packed.at[b, v], packed.at[b, v], psend.at[v, d], precv.at[v, N_LINE - d], at_px(d)
            )
            for d in FAR_FIRST
        ]
        for v in range(2)
    ]
    gather_tiles(0)
    for copy in p_copies[0]:
        copy.start()

    gather_tiles(1)
    for copy in p_copies[1]:
        copy.start()

    names = jnp.concatenate(
        [column[lax.rem(a + d, N_LINE), SLICE:SLICE + 8] for d in range(N_LINE)], axis=0
    )
    wanted = jnp.concatenate([names, names], axis=0).T
    lane = lax.broadcasted_iota(jnp.int32, (1, LINE), 1)
    tile = (lane >= 128).astype(jnp.int32) + (lane >= 256).astype(jnp.int32)
    lane = lane - 128 * tile
    place = (lane >= CELLS).astype(jnp.int32) + (lane >= 2 * CELLS).astype(jnp.int32)
    owner = 3 * tile + place
    stored = owner * (N_LINE * CELLS) + (lane - CELLS * place)
    held = (lane < 3 * CELLS) & (owner < N_LINE)
    stored = jnp.concatenate(
        [jnp.where(held, stored + CELLS * n, -2) for n in range(N_LINE)], axis=1
    ).astype(f32)
    for v in range(2):
        for d in range(0, N_LINE, 2):
            hot[v, PAD * d:PAD * (d + 2)] = jnp.concatenate(
                [
                    jnp.where(wanted[0:PAD, 8 * n + v:8 * n + v + 1] == stored, 1.0, 0.0)
                    for n in (d, d + 1)
                ],
                axis=0,
            ).astype(bf16)

    inputs[4].wait()
    h_down.wait_recv()
    h_up.wait_recv()

    @pl.when(a == 0)
    def _():
        ext[:, 0:BORDER, :] = jnp.zeros((2, BORDER, SIDE), f32)

    @pl.when(a == N_LINE - 1)
    def _():
        ext[:, BORDER + SIDE:ROWS, :] = jnp.zeros((2, BORDER, SIDE), f32)

    def pack(v, carry):
        lane = lanes(CHUNK)
        last = jnp.zeros((CHUNK, 128), f32)
        first = jnp.zeros((CHUNK, 128), f32)
        for g in range(ROWS // CHUNK):
            inside = (lane >= HALF * g) & (lane < HALF * (g + 1))
            rows = slice(CHUNK * g, CHUNK * (g + 1))
            last = jnp.where(inside, turn(ext[v, rows, 256:384], HALF * g - 108), last)
            first = jnp.where(inside, turn(ext[v, rows, 0:128], HALF * g), first)
        xs[0, v] = last
        xs[1, v] = first
        return carry

    lax.fori_loop(0, 2, pack, 0)
    x_copies = [
        remote(xs.at[0], xr.at[0], xsend.at[0], xrecv.at[0], at_px(1)),
        remote(xs.at[1], xr.at[1], xsend.at[1], xrecv.at[1], at_px(N_LINE - 1)),
    ]
    for copy in x_copies:
        copy.start()

    s_copies = [
        [
            remote(
                sbuf.at[v, d], rbuf.at[v, a], ssend.at[v, d], srecv.at[v, N_LINE - d], at_py(d)
            )
            for d in FAR_FIRST
        ]
        for v in range(2)
    ]

    def pick(v):
        for copy in p_copies[v]:
            copy.wait_recv()
        high, low = split(jnp.concatenate([packed[n, v] for n in range(N_LINE)], axis=1))
        table = jnp.concatenate([high, low, jnp.zeros((64, STORE), bf16)], axis=0)
        picked = lax.dot_general(
            hot[v], table, (((1,), (1,)), ((), ())), preferred_element_type=f32
        )
        picked = picked + turn(picked, -SLICE)
        groups = picked.reshape(N_LINE, 5, 8, 128)
        groups = [groups[:, g].reshape(8 * N_LINE, 128) for g in range(5)]
        lane = lanes(8 * N_LINE)
        first = groups[0]
        for g in range(1, 4):
            first = jnp.where(lane < SLICE * g, first, turn(groups[g], SLICE * g))
        sbuf[v, :, 0:8] = first.reshape(N_LINE, 8, 128)
        sbuf[v, :, 8:16] = groups[4].reshape(N_LINE, 8, 128)
        rbuf[v, a] = sbuf[v, 0]
        for copy in s_copies[v]:
            copy.start()

    pick(0)
    pick(1)

    for copy in x_copies:
        copy.wait_recv()

    def tiles(v):
        tall = 2 * CHUNK
        lane = lanes(tall)
        for j in range(ROWS // tall):
            rows = slice(tall * j, tall * (j + 1))
            raw = [ext[v, rows, 128 * d:128 * (d + 1)] for d in range(3)]
            even = [turn(t, HALF) for t in raw]
            odd = [turn(t, 84) for t in raw]
            border = xr[0, v]
            left = jnp.concatenate(
                [turn(border, -HALF * g) for g in (2 * j, 2 * j + 1)], axis=0
            )
            left = jnp.where(b == 0, 0.0, left)
            border = xr[1, v]
            right = jnp.concatenate(
                [turn(border, 84 - HALF * g) for g in (2 * j, 2 * j + 1)], axis=0
            )
            right = jnp.where(b == N_LINE - 1, 0.0, right)
            before = [left] + even
            after = odd + [right]
            for d in range(3):
                high, low = split(jnp.where(lane < HALF, before[d], even[d]))
                thi[v, 2 * d, rows] = high
                tlo[v, 2 * d, rows] = low
                high, low = split(jnp.where(lane < 84, odd[d], after[d + 1]))
                thi[v, 2 * d + 1, rows] = high
                tlo[v, 2 * d + 1, rows] = low

    tiles(0)
    tiles(1)

    half = CELL // 2

    def receive_taps(v):
        for copy in s_copies[v]:
            copy.wait_recv()
        lane = lanes(8)
        total = []
        for n in range(2):
            groups = []
            for g in range(5):
                rows, shift = (slice(0, 8), SLICE * g) if g < 4 else (slice(8, 16), 0)
                piece = turn(rbuf[v, 4 * n, rows], -shift)
                for i in range(1, 4):
                    other = turn(rbuf[v, 4 * n + i, rows], SLICE * i - shift)
                    piece = jnp.where(lane < SLICE * i, piece, other)
                groups.append(piece)
            total.append(jnp.concatenate(groups, axis=0))
        lane = lanes(PAD)
        pieces = ([], [])
        for p in range(2 * RANK):
            n, offset = divmod(TAPS * p, 128)
            tap = turn(total[n], -offset)
            if offset + TAPS > 128:
                rest = turn(total[n + 1], -offset)
                tap = jnp.where(lane < 128 - offset, tap, rest)
            tap = jnp.where(lane < TAPS, tap, 0.0)
            high = tap.astype(bf16).astype(f32)
            pieces[p % 2].extend((high, tap - high))
        spot = lax.broadcasted_iota(jnp.int32, (128, 128), 0) + lanes(128)
        mirror = jnp.where((spot == 0) | (spot == 128), 1.0, 0.0).astype(bf16)
        turned = jnp.dot(
            jnp.concatenate(pieces[1], axis=0).astype(bf16), mirror, preferred_element_type=f32
        )
        for k in range(RANK):
            for part in range(2):
                n = 2 * k + part
                taps[v, 2 * k, part] = pieces[0][n]
                taps[v, 2 * k + 1, part] = turned[PAD * n:PAD * (n + 1)]

    def band(v, p, part, q, count, shift):
        row = jnp.broadcast_to(taps[v, p, part, pl.ds(q, 1), :], (count, 128))
        return pltpu.roll(row, shift, 1, stride=1, stride_axis=0)

    def row_bands(v, q):
        lane = lanes(half)
        parts = []
        for k in range(RANK):
            near = band(v, 2 * k, 0, q, half, 4)
            low = band(v, 2 * k, 1, q, half, WINDOW + 4)
            far = band(v, 2 * k, 0, q, half, 2 * WINDOW + 4 - 128)
            parts.append(
                jnp.concatenate(
                    [
                        jnp.where(lane < WINDOW, near, low),
                        jnp.where(lane < 2 * WINDOW - 128, low, far),
                    ],
                    axis=1,
                )
            )
        return jnp.concatenate(parts, axis=0).astype(bf16)

    def col_bands(v, q):
        reach = CELL + 2 * HALF
        parts = []
        for k in range(RANK):
            high = band(v, 2 * k + 1, 0, q, reach, 0)
            low = band(v, 2 * k + 1, 1, q, reach, CELL)
            parts += [
                jnp.where(lanes(reach) < CELL, high, low), jnp.zeros((128 - reach, 128), f32)
            ]
        return jnp.concatenate(parts, axis=0).astype(bf16)

    def visit_and_row(step):
        late = step // (2 * EACH)
        visit = (1 - late) * (step // EACH) + late * lax.rem(step, 2)
        place = (1 - late) * lax.rem(step, EACH) + late * (step // 2)
        near = place // 3
        place = place - 3 * near
        flip = lax.rem(x + near, 2)
        place = place + flip * (2 - 2 * place)
        side = x // 2
        return visit, 3 * ((1 - side) * (1 - near) + side * near) + place

    def row_pass(step):
        v, r = visit_and_row(step)
        top = pl.multiple_of(r * CELL, CELL)
        for c in range(CPS):
            windows = []
            for h in range(2):
                rows = pl.ds(pl.multiple_of(top + half * h, half), WINDOW)
                high = thi[v, c, rows, :]
                windows.append(
                    jnp.concatenate([high, high, tlo[v, c, rows, :], high[0:16]], axis=0)
                )
            part = jnp.dot(
                row_bands(v, r * CPS + c), jnp.concatenate(windows, axis=1),
                preferred_element_type=f32,
            )
            halves[lax.rem(step, 2) * CPS + c] = jnp.concatenate(
                [
                    jnp.concatenate(
                        [
                            piece[half * k:half * (k + 1), 128 * h:128 * (h + 1)]
                            for k in range(RANK)
                        ],
                        axis=1,
                    )
                    for piece in split(part)
                    for h in range(2)
                ],
                axis=0,
            )

    def col_pass(step):
        v, r = visit_and_row(step)
        rows = pl.ds(pl.multiple_of(r * CELL, CELL), CELL)
        for c in range(0, CPS, 2):
            pair = []
            for n in (c, c + 1):
                both = jnp.dot(
                    halves[lax.rem(step, 2) * CPS + n], col_bands(v, r * CPS + n),
                    preferred_element_type=f32,
                )
                both = both[0:CELL] + both[CELL:2 * CELL]
                pair.append(both + turn(both, CELL))
            cols = slice(CELL * c, CELL * c + 128)
            term = weight[v, rows, cols] * jnp.where(lanes(CELL) < CELL, pair[0], pair[1])
            num[rows, cols] = num[rows, cols] + term

    num_copies = [
        share_part(0, 0, 64, 0), share_part(0, 64, 32, 1), share_part(1, 0, 96, 2),
        share_part(2, 0, 64, 3), share_part(2, 64, 32, 4),
    ]

    receive_taps(0)
    row_pass(jnp.int32(0))

    @pl.loop(1, EACH)
    def _(step):
        row_pass(step)
        col_pass(step - 1)

    receive_taps(1)

    @pl.loop(EACH, 2 * CPS)
    def _(step):
        row_pass(step)
        col_pass(step - 1)
        for copy, ready in zip(num_copies, (5, 6, 7, 8, 10)):

            @pl.when(step == ready)
            def _():
                copy.start()

    col_pass(jnp.int32(2 * CPS - 1))

    mine = pl.ds(pl.multiple_of(x * SHARE, SHARE), SHARE)
    for copy in den_copies + num_copies:
        copy.wait_recv()
    weight_sum[...] = (den[mine] + rden[1]) + (rden[0] + rden[2])
    top_sum[...] = (num[mine] + rnum[1]) + (rnum[0] + rnum[2])

    for copy in z_copies + [h_down, h_up] + x_copies + p_copies[0] + p_copies[1]:
        copy.wait_send()
    for copy in s_copies[0] + s_copies[1] + den_copies + num_copies:
        copy.wait_send()


def shards(warped_image, variance, kernel_factors, cell_source, coverage):
    vmem = pl.BlockSpec(memory_space=pltpu.VMEM)
    dma = pltpu.SemaphoreType.DMA
    out = jax.ShapeDtypeStruct((SHARE, SIDE), f32)
    top_sum, weight_sum = pl.pallas_call(
        kernel,
        out_shape=(out, out),
        in_specs=[pl.BlockSpec(memory_space=pl.ANY)] * 5,
        out_specs=(vmem, vmem),
        scratch_shapes=[
            pltpu.VMEM((2, ROWS, SIDE), f32),
            pltpu.VMEM((2, SIDE, SIDE), f32),
            pltpu.VMEM((CELLS, 2, FACT), f32),
            pltpu.VMEM((2, CELLS), jnp.int32),
            pltpu.SMEM((2, CELLS), jnp.int32),
            pltpu.VMEM((128, 256), f32),
            pltpu.VMEM((N_LINE, SLICE + 8, 128), f32),
            pltpu.VMEM((N_LINE, SLICE + 8, 128), f32),
            pltpu.VMEM((N_LINE, 2, SLICE, LINE), f32),
            pltpu.VMEM((2, N_LINE * PAD, STORE), bf16),
            pltpu.VMEM((2, N_LINE, 16, 128), f32),
            pltpu.VMEM((2, N_LINE, 16, 128), f32),
            pltpu.VMEM((2, 2 * RANK, 2, PAD, 128), f32),
            pltpu.VMEM((2, 2, CHUNK, 128), f32),
            pltpu.VMEM((2, 2, CHUNK, 128), f32),
            pltpu.VMEM((2, CPS, ROWS, 128), bf16),
            pltpu.VMEM((2, CPS, ROWS, 128), bf16),
            pltpu.VMEM((2, SIDE, SIDE), f32),
            pltpu.VMEM((SIDE, SIDE), f32),
            pltpu.VMEM((SIDE, SIDE), f32),
            pltpu.VMEM((N_VERT - 1, SHARE, SIDE), f32),
            pltpu.VMEM((N_VERT - 1, SHARE, SIDE), f32),
            pltpu.VMEM((2 * CPS, 128, 384), bf16),
            dma((5,)),
            dma((N_LINE,)), dma((N_LINE,)),
            dma((2, N_LINE)), dma((2, N_LINE)),
            dma((2, N_LINE)), dma((2, N_LINE)),
            dma((2,)), dma((2,)), dma((2,)), dma((2,)),
            dma((5,)), dma((5,)), dma((3,)), dma((3,)),
        ],
        compiler_params=pltpu.CompilerParams(
            collective_id=0, has_side_effects=True, vmem_limit_bytes=60 * 1024 * 1024
        ),
    )(warped_image, variance, kernel_factors.transpose(1, 0, 2), cell_source, coverage)
    weight_sum = jnp.maximum(weight_sum, 0.5)
    return top_sum / weight_sum, weight_sum


def solution(mesh):
    placed = (
        P("vert", "py", "px"),
        P("vert", "py", "px"),
        P("vert", ("py", "px"), None),
        P("vert", ("py", "px")),
        P("vert", ("py", "px")),
    )
    return jax.shard_map(
        shards,
        mesh=mesh,
        in_specs=placed,
        out_specs=(P(("py", "vert"), "px"), P(("py", "vert"), "px")),
        check_vma=False,
    )
```

```python
import jax
import jax.numpy as jnp
from jax import lax
from jax.experimental import pallas as pl
from jax.experimental.pallas import tpu as pltpu
from jax.sharding import PartitionSpec as P

TAPS = 41
RANK = 3
CELL = 64
HALF = 20
CPS = 6
SIDE = 384
CELLS = 36
PAD = 40
FACT = 246
BORDER = 24
ROWS = SIDE + 2 * BORDER
WINDOW = 80
SHARE = 96
EACH = 4
SLICE = 32
LINE = 384
CHUNK = 72
N_VERT = 4
N_LINE = 8
FAR_FIRST = (4, 5, 3, 6, 2, 7, 1)
STORE = N_LINE * LINE

MESH = pl.DeviceIdType.MESH
f32 = jnp.float32
bf16 = jnp.bfloat16


def lanes(rows):
    return lax.broadcasted_iota(jnp.int32, (rows, 128), 1)


def turn(x, shift):
    shift = shift % 128
    return x if shift == 0 else pltpu.roll(x, shift, 1)


def split(x):
    high = x.astype(bf16)
    low = (x - high.astype(f32)).astype(bf16)
    return high, low


def kernel(
    img, var_in, fac_in, cs_in, cov_in,
    top_sum, weight_sum,
    ext, var, fac, cs, cov, cells, slices, column, packed, hot, sbuf, rbuf, taps, xs, xr, thi, tlo, weight, num, den,
    rnum, rden, halves,
    in_sem, zsend, zrecv, psend, precv, ssend, srecv, hsend, hrecv, xsend, xrecv,
    nsend, nrecv, dsend, drecv,
):
    a = lax.axis_index("py")
    b = lax.axis_index("px")
    x = lax.axis_index("vert")
    others = (lax.rem(x + 2, N_VERT), N_VERT - 1 - x, x + 1 - 2 * lax.rem(x, 2))

    def at_py(d):
        return {"py": lax.rem(a + d, N_LINE)}

    def at_px(d):
        return {"px": lax.rem(b + d, N_LINE)}

    def remote(src, dst, send, recv, device):
        return pltpu.make_async_remote_copy(
            src_ref=src, dst_ref=dst, send_sem=send, recv_sem=recv,
            device_id=device, device_id_type=MESH,
        )

    barrier = pltpu.get_barrier_semaphore()
    for d in FAR_FIRST:
        pl.semaphore_signal(barrier, inc=1, device_id=at_py(d), device_id_type=MESH)
    for d in range(1, N_LINE):
        pl.semaphore_signal(barrier, inc=1, device_id=at_px(d), device_id_type=MESH)
    for target in others:
        pl.semaphore_signal(barrier, inc=1, device_id={"vert": target}, device_id_type=MESH)

    inputs = [
        pltpu.make_async_copy(source, target, in_sem.at[n])
        for n, (source, target) in enumerate((
            (fac_in, fac), (cs_in, cs), (cov_in, cov), (var_in, var),
            (img, ext.at[:, pl.ds(BORDER, SIDE), :]),
        ))
    ]
    for copy in inputs:
        copy.start()

    inputs[0].wait()
    cells[...] = jnp.zeros((128, 256), f32)
    for v in range(2):
        cells[CELLS * v:CELLS * (v + 1), 0:FACT] = fac[:, v, :]
    for n in range(2):
        slices[4 * n:4 * (n + 1), 0:SLICE] = cells[:, 128 * n:128 * (n + 1)].T.reshape(4, SLICE, 128)
    inputs[1].wait()
    slices[:, SLICE:SLICE + 8] = jnp.full((N_LINE, 8, 128), -1.0, f32)
    for n in range(N_LINE):
        slices[n, SLICE:SLICE + 2, 0:CELLS] = cs[...].astype(f32)
    column[a] = slices[a]

    pl.semaphore_wait(barrier, 2 * (N_LINE - 1) + N_VERT - 1)

    z_copies = [
        remote(
            slices.at[lax.rem(a + d, N_LINE)], column.at[a], zsend.at[d], zrecv.at[N_LINE - d],
            at_py(d),
        )
        for d in FAR_FIRST
    ]
    h_down = remote(
        img.at[:, pl.ds(SIDE - BORDER, BORDER), :], ext.at[:, pl.ds(0, BORDER), :],
        hsend.at[0], hrecv.at[0], at_py(1),
    )
    h_up = remote(
        img.at[:, pl.ds(0, BORDER), :], ext.at[:, pl.ds(BORDER + SIDE, BORDER), :],
        hsend.at[1], hrecv.at[1], at_py(N_LINE - 1),
    )
    for copy in z_copies + [h_down, h_up]:
        copy.start()

    inputs[2].wait()
    inputs[3].wait()

    def weight_rows(r, carry):
        rows = pl.ds(pl.multiple_of(r * CELL, CELL), CELL)
        lane = lanes(CELL)
        for c in range(CPS // 2):
            cols = pl.ds(128 * c, 128)
            total = jnp.zeros((CELL, 128), f32)
            for v in range(2):
                left = cov[v, r * CPS + 2 * c].astype(f32)
                right = cov[v, r * CPS + 2 * c + 1].astype(f32)
                w = jnp.where(lane < CELL, left, right) / var[v, rows, cols]
                weight[v, rows, cols] = w
                total = total + w
            den[rows, cols] = total
            num[rows, cols] = jnp.zeros((CELL, 128), f32)
        return carry

    lax.fori_loop(0, CPS, weight_rows, 0)

    def share(ref, t):
        return ref.at[pl.ds(pl.multiple_of(t * SHARE, SHARE), SHARE)]

    den_copies = [
        remote(share(den, t), rden.at[n], dsend.at[n], drecv.at[n], {"vert": t})
        for n, t in enumerate(others)
    ]
    for copy in den_copies:
        copy.start()

    def share_part(n, first, count, sem):
        t = others[n]
        first = first + lax.rem(t, 2) * (SHARE - count - 2 * first)
        first = pl.multiple_of(first, 32)
        base = pl.multiple_of(t * SHARE + first, 32)
        return remote(
            num.at[pl.ds(base, count)], rnum.at[n, pl.ds(first, count)],
            nsend.at[sem], nrecv.at[sem], {"vert": t},
        )

    for copy in z_copies:
        copy.wait_recv()
    lane = lanes(SLICE)

    def gather_tiles(v):
        for t in range(3):
            tile = jnp.zeros((SLICE, 128), f32)
            for i in range(min(3, N_LINE - 3 * t)):
                inside = (lane >= CELLS * i) & (lane < CELLS * (i + 1))
                part = turn(column[3 * t + i, 0:SLICE], CELLS * (i - v))
                tile = jnp.where(inside, part, tile)
            packed[b, v, :, 128 * t:128 * (t + 1)] = tile

    p_copies = [
        [
            remote(
                packed.at[b, v], packed.at[b, v], psend.at[v, d], precv.at[v, N_LINE - d], at_px(d)
            )
            for d in FAR_FIRST
        ]
        for v in range(2)
    ]
    gather_tiles(0)
    for copy in p_copies[0]:
        copy.start()

    gather_tiles(1)
    for copy in p_copies[1]:
        copy.start()

    names = jnp.concatenate(
        [column[lax.rem(a + d, N_LINE), SLICE:SLICE + 8] for d in range(N_LINE)], axis=0
    )
    wanted = jnp.concatenate([names, names], axis=0).T
    lane = lax.broadcasted_iota(jnp.int32, (1, LINE), 1)
    tile = (lane >= 128).astype(jnp.int32) + (lane >= 256).astype(jnp.int32)
    lane = lane - 128 * tile
    place = (lane >= CELLS).astype(jnp.int32) + (lane >= 2 * CELLS).astype(jnp.int32)
    owner = 3 * tile + place
    stored = owner * (N_LINE * CELLS) + (lane - CELLS * place)
    held = (lane < 3 * CELLS) & (owner < N_LINE)
    stored = jnp.concatenate(
        [jnp.where(held, stored + CELLS * n, -2) for n in range(N_LINE)], axis=1
    ).astype(f32)
    for v in range(2):
        for d in range(0, N_LINE, 2):
            hot[v, PAD * d:PAD * (d + 2)] = jnp.concatenate(
                [
                    jnp.where(wanted[0:PAD, 8 * n + v:8 * n + v + 1] == stored, 1.0, 0.0)
                    for n in (d, d + 1)
                ],
                axis=0,
            ).astype(bf16)

    inputs[4].wait()
    h_down.wait_recv()
    h_up.wait_recv()

    @pl.when(a == 0)
    def _():
        ext[:, 0:BORDER, :] = jnp.zeros((2, BORDER, SIDE), f32)

    @pl.when(a == N_LINE - 1)
    def _():
        ext[:, BORDER + SIDE:ROWS, :] = jnp.zeros((2, BORDER, SIDE), f32)

    def pack(v, carry):
        lane = lanes(CHUNK)
        last = jnp.zeros((CHUNK, 128), f32)
        first = jnp.zeros((CHUNK, 128), f32)
        for g in range(ROWS // CHUNK):
            inside = (lane >= HALF * g) & (lane < HALF * (g + 1))
            rows = slice(CHUNK * g, CHUNK * (g + 1))
            last = jnp.where(inside, turn(ext[v, rows, 256:384], HALF * g - 108), last)
            first = jnp.where(inside, turn(ext[v, rows, 0:128], HALF * g), first)
        xs[0, v] = last
        xs[1, v] = first
        return carry

    lax.fori_loop(0, 2, pack, 0)
    x_copies = [
        remote(xs.at[0], xr.at[0], xsend.at[0], xrecv.at[0], at_px(1)),
        remote(xs.at[1], xr.at[1], xsend.at[1], xrecv.at[1], at_px(N_LINE - 1)),
    ]
    for copy in x_copies:
        copy.start()

    s_copies = [
        [
            remote(
                sbuf.at[v, d], rbuf.at[v, a], ssend.at[v, d], srecv.at[v, N_LINE - d], at_py(d)
            )
            for d in FAR_FIRST
        ]
        for v in range(2)
    ]

    def pick(v):
        for copy in p_copies[v]:
            copy.wait_recv()
        high, low = split(jnp.concatenate([packed[n, v] for n in range(N_LINE)], axis=1))
        table = jnp.concatenate([high, low, jnp.zeros((64, STORE), bf16)], axis=0)
        picked = lax.dot_general(
            hot[v], table, (((1,), (1,)), ((), ())), preferred_element_type=f32
        )
        picked = picked + turn(picked, -SLICE)
        groups = picked.reshape(N_LINE, 5, 8, 128)
        groups = [groups[:, g].reshape(8 * N_LINE, 128) for g in range(5)]
        lane = lanes(8 * N_LINE)
        first = groups[0]
        for g in range(1, 4):
            first = jnp.where(lane < SLICE * g, first, turn(groups[g], SLICE * g))
        sbuf[v, :, 0:8] = first.reshape(N_LINE, 8, 128)
        sbuf[v, :, 8:16] = groups[4].reshape(N_LINE, 8, 128)
        rbuf[v, a] = sbuf[v, 0]
        for copy in s_copies[v]:
            copy.start()

    pick(0)
    pick(1)

    for copy in x_copies:
        copy.wait_recv()

    def tiles(v):
        tall = 2 * CHUNK
        lane = lanes(tall)
        for j in range(ROWS // tall):
            rows = slice(tall * j, tall * (j + 1))
            raw = [ext[v, rows, 128 * d:128 * (d + 1)] for d in range(3)]
            even = [turn(t, HALF) for t in raw]
            odd = [turn(t, 84) for t in raw]
            border = xr[0, v]
            left = jnp.concatenate(
                [turn(border, -HALF * g) for g in (2 * j, 2 * j + 1)], axis=0
            )
            left = jnp.where(b == 0, 0.0, left)
            border = xr[1, v]
            right = jnp.concatenate(
                [turn(border, 84 - HALF * g) for g in (2 * j, 2 * j + 1)], axis=0
            )
            right = jnp.where(b == N_LINE - 1, 0.0, right)
            before = [left] + even
            after = odd + [right]
            for d in range(3):
                high, low = split(jnp.where(lane < HALF, before[d], even[d]))
                thi[v, 2 * d, rows] = high
                tlo[v, 2 * d, rows] = low
                high, low = split(jnp.where(lane < 84, odd[d], after[d + 1]))
                thi[v, 2 * d + 1, rows] = high
                tlo[v, 2 * d + 1, rows] = low

    tiles(0)
    tiles(1)

    half = CELL // 2

    def receive_taps(v):
        for copy in s_copies[v]:
            copy.wait_recv()
        lane = lanes(8)
        total = []
        for n in range(2):
            groups = []
            for g in range(5):
                rows, shift = (slice(0, 8), SLICE * g) if g < 4 else (slice(8, 16), 0)
                piece = turn(rbuf[v, 4 * n, rows], -shift)
                for i in range(1, 4):
                    other = turn(rbuf[v, 4 * n + i, rows], SLICE * i - shift)
                    piece = jnp.where(lane < SLICE * i, piece, other)
                groups.append(piece)
            total.append(jnp.concatenate(groups, axis=0))
        lane = lanes(PAD)
        pieces = ([], [])
        for p in range(2 * RANK):
            n, offset = divmod(TAPS * p, 128)
            tap = turn(total[n], -offset)
            if offset + TAPS > 128:
                rest = turn(total[n + 1], -offset)
                tap = jnp.where(lane < 128 - offset, tap, rest)
            tap = jnp.where(lane < TAPS, tap, 0.0)
            high = tap.astype(bf16).astype(f32)
            pieces[p % 2].extend((high, tap - high))
        spot = lax.broadcasted_iota(jnp.int32, (128, 128), 0) + lanes(128)
        mirror = jnp.where((spot == 0) | (spot == 128), 1.0, 0.0).astype(bf16)
        turned = jnp.dot(
            jnp.concatenate(pieces[1], axis=0).astype(bf16), mirror, preferred_element_type=f32
        )
        for k in range(RANK):
            for part in range(2):
                n = 2 * k + part
                taps[v, 2 * k, part] = pieces[0][n]
                taps[v, 2 * k + 1, part] = turned[PAD * n:PAD * (n + 1)]

    def band(v, p, part, q, count, shift):
        row = jnp.broadcast_to(taps[v, p, part, pl.ds(q, 1), :], (count, 128))
        return pltpu.roll(row, shift, 1, stride=1, stride_axis=0)

    def row_bands(v, q):
        lane = lanes(half)
        parts = []
        for k in range(RANK):
            near = band(v, 2 * k, 0, q, half, 4)
            low = band(v, 2 * k, 1, q, half, WINDOW + 4)
            far = band(v, 2 * k, 0, q, half, 2 * WINDOW + 4 - 128)
            parts.append(
                jnp.concatenate(
                    [
                        jnp.where(lane < WINDOW, near, low),
                        jnp.where(lane < 2 * WINDOW - 128, low, far),
                    ],
                    axis=1,
                )
            )
        return jnp.concatenate(parts, axis=0).astype(bf16)

    def col_bands(v, q):
        reach = CELL + 2 * HALF
        parts = []
        for k in range(RANK):
            high = band(v, 2 * k + 1, 0, q, reach, 0)
            low = band(v, 2 * k + 1, 1, q, reach, CELL)
            parts += [
                jnp.where(lanes(reach) < CELL, high, low), jnp.zeros((128 - reach, 128), f32)
            ]
        return jnp.concatenate(parts, axis=0).astype(bf16)

    def visit_and_row(step):
        late = step // (2 * EACH)
        visit = (1 - late) * (step // EACH) + late * lax.rem(step, 2)
        place = (1 - late) * lax.rem(step, EACH) + late * (step // 2)
        near = place // 3
        place = place - 3 * near
        flip = lax.rem(x + near, 2)
        place = place + flip * (2 - 2 * place)
        side = x // 2
        return visit, 3 * ((1 - side) * (1 - near) + side * near) + place

    def row_pass(step):
        v, r = visit_and_row(step)
        top = pl.multiple_of(r * CELL, CELL)
        for c in range(CPS):
            windows = []
            for h in range(2):
                rows = pl.ds(pl.multiple_of(top + half * h, half), WINDOW)
                high = thi[v, c, rows, :]
                windows.append(
                    jnp.concatenate([high, high, tlo[v, c, rows, :], high[0:16]], axis=0)
                )
            part = jnp.dot(
                row_bands(v, r * CPS + c), jnp.concatenate(windows, axis=1),
                preferred_element_type=f32,
            )
            halves[lax.rem(step, 2) * CPS + c] = jnp.concatenate(
                [
                    jnp.concatenate(
                        [
                            piece[half * k:half * (k + 1), 128 * h:128 * (h + 1)]
                            for k in range(RANK)
                        ],
                        axis=1,
                    )
                    for piece in split(part)
                    for h in range(2)
                ],
                axis=0,
            )

    def col_pass(step):
        v, r = visit_and_row(step)
        rows = pl.ds(pl.multiple_of(r * CELL, CELL), CELL)
        for c in range(0, CPS, 2):
            pair = []
            for n in (c, c + 1):
                both = jnp.dot(
                    halves[lax.rem(step, 2) * CPS + n], col_bands(v, r * CPS + n),
                    preferred_element_type=f32,
                )
                both = both[0:CELL] + both[CELL:2 * CELL]
                pair.append(both + turn(both, CELL))
            cols = slice(CELL * c, CELL * c + 128)
            term = weight[v, rows, cols] * jnp.where(lanes(CELL) < CELL, pair[0], pair[1])
            num[rows, cols] = num[rows, cols] + term

    num_copies = [
        share_part(0, 0, 64, 0), share_part(0, 64, 32, 1), share_part(1, 64, 32, 2),
        share_part(1, 0, 64, 3), share_part(2, 0, 64, 4), share_part(2, 64, 32, 5),
    ]

    receive_taps(0)
    row_pass(jnp.int32(0))

    @pl.loop(1, EACH)
    def _(step):
        row_pass(step)
        col_pass(step - 1)

    receive_taps(1)

    @pl.loop(EACH, 2 * CPS)
    def _(step):
        row_pass(step)
        col_pass(step - 1)
        for copy, ready in zip(num_copies, (5, 6, 6, 7, 8, 10)):

            @pl.when(step == ready)
            def _():
                copy.start()

    col_pass(jnp.int32(2 * CPS - 1))

    mine = pl.ds(pl.multiple_of(x * SHARE, SHARE), SHARE)
    for copy in den_copies + num_copies:
        copy.wait_recv()
    weight_sum[...] = (den[mine] + rden[1]) + (rden[0] + rden[2])
    top_sum[...] = (num[mine] + rnum[1]) + (rnum[0] + rnum[2])

    for copy in z_copies + [h_down, h_up] + x_copies + p_copies[0] + p_copies[1]:
        copy.wait_send()
    for copy in s_copies[0] + s_copies[1] + den_copies + num_copies:
        copy.wait_send()


def shards(warped_image, variance, kernel_factors, cell_source, coverage):
    vmem = pl.BlockSpec(memory_space=pltpu.VMEM)
    dma = pltpu.SemaphoreType.DMA
    out = jax.ShapeDtypeStruct((SHARE, SIDE), f32)
    top_sum, weight_sum = pl.pallas_call(
        kernel,
        out_shape=(out, out),
        in_specs=[pl.BlockSpec(memory_space=pl.ANY)] * 5,
        out_specs=(vmem, vmem),
        scratch_shapes=[
            pltpu.VMEM((2, ROWS, SIDE), f32),
            pltpu.VMEM((2, SIDE, SIDE), f32),
            pltpu.VMEM((CELLS, 2, FACT), f32),
            pltpu.VMEM((2, CELLS), jnp.int32),
            pltpu.SMEM((2, CELLS), jnp.int32),
            pltpu.VMEM((128, 256), f32),
            pltpu.VMEM((N_LINE, SLICE + 8, 128), f32),
            pltpu.VMEM((N_LINE, SLICE + 8, 128), f32),
            pltpu.VMEM((N_LINE, 2, SLICE, LINE), f32),
            pltpu.VMEM((2, N_LINE * PAD, STORE), bf16),
            pltpu.VMEM((2, N_LINE, 16, 128), f32),
            pltpu.VMEM((2, N_LINE, 16, 128), f32),
            pltpu.VMEM((2, 2 * RANK, 2, PAD, 128), f32),
            pltpu.VMEM((2, 2, CHUNK, 128), f32),
            pltpu.VMEM((2, 2, CHUNK, 128), f32),
            pltpu.VMEM((2, CPS, ROWS, 128), bf16),
            pltpu.VMEM((2, CPS, ROWS, 128), bf16),
            pltpu.VMEM((2, SIDE, SIDE), f32),
            pltpu.VMEM((SIDE, SIDE), f32),
            pltpu.VMEM((SIDE, SIDE), f32),
            pltpu.VMEM((N_VERT - 1, SHARE, SIDE), f32),
            pltpu.VMEM((N_VERT - 1, SHARE, SIDE), f32),
            pltpu.VMEM((2 * CPS, 128, 384), bf16),
            dma((5,)),
            dma((N_LINE,)), dma((N_LINE,)),
            dma((2, N_LINE)), dma((2, N_LINE)),
            dma((2, N_LINE)), dma((2, N_LINE)),
            dma((2,)), dma((2,)), dma((2,)), dma((2,)),
            dma((6,)), dma((6,)), dma((3,)), dma((3,)),
        ],
        compiler_params=pltpu.CompilerParams(
            collective_id=0, has_side_effects=True, vmem_limit_bytes=60 * 1024 * 1024
        ),
    )(warped_image, variance, kernel_factors.transpose(1, 0, 2), cell_source, coverage)
    weight_sum = jnp.maximum(weight_sum, 0.5)
    return top_sum / weight_sum, weight_sum


def solution(mesh):
    placed = (
        P("vert", "py", "px"),
        P("vert", "py", "px"),
        P("vert", ("py", "px"), None),
        P("vert", ("py", "px")),
        P("vert", ("py", "px")),
    )
    return jax.shard_map(
        shards,
        mesh=mesh,
        in_specs=placed,
        out_specs=(P(("py", "vert"), "px"), P(("py", "vert"), "px")),
        check_vma=False,
    )
```

```python
import jax
import jax.numpy as jnp
from jax import lax
from jax.experimental import pallas as pl
from jax.experimental.pallas import tpu as pltpu
from jax.sharding import PartitionSpec as P

TAPS = 41
RANK = 3
CELL = 64
HALF = 20
CPS = 6
SIDE = 384
CELLS = 36
PAD = 40
FACT = 246
BORDER = 24
ROWS = SIDE + 2 * BORDER
WINDOW = 80
SHARE = 96
EACH = 5
SLICE = 32
LINE = 384
CHUNK = 72
N_VERT = 4
N_LINE = 8
FAR_FIRST = (4, 5, 3, 6, 2, 7, 1)
STORE = N_LINE * LINE

MESH = pl.DeviceIdType.MESH
f32 = jnp.float32
bf16 = jnp.bfloat16


def lanes(rows):
    return lax.broadcasted_iota(jnp.int32, (rows, 128), 1)


def turn(x, shift):
    shift = shift % 128
    return x if shift == 0 else pltpu.roll(x, shift, 1)


def split(x):
    high = x.astype(bf16)
    low = (x - high.astype(f32)).astype(bf16)
    return high, low


def kernel(
    img, var_in, fac_in, cs_in, cov_in,
    top_sum, weight_sum,
    ext, var, fac, cs, cov, cells, slices, column, packed, hot, sbuf, rbuf, taps, xs, xr, thi, tlo, weight, num, den,
    rnum, rden, halves,
    in_sem, zsend, zrecv, psend, precv, ssend, srecv, hsend, hrecv, xsend, xrecv,
    nsend, nrecv, dsend, drecv,
):
    a = lax.axis_index("py")
    b = lax.axis_index("px")
    x = lax.axis_index("vert")
    others = (lax.rem(x + 2, N_VERT), N_VERT - 1 - x, x + 1 - 2 * lax.rem(x, 2))

    def at_py(d):
        return {"py": lax.rem(a + d, N_LINE)}

    def at_px(d):
        return {"px": lax.rem(b + d, N_LINE)}

    def remote(src, dst, send, recv, device):
        return pltpu.make_async_remote_copy(
            src_ref=src, dst_ref=dst, send_sem=send, recv_sem=recv,
            device_id=device, device_id_type=MESH,
        )

    barrier = pltpu.get_barrier_semaphore()
    for d in FAR_FIRST:
        pl.semaphore_signal(barrier, inc=1, device_id=at_py(d), device_id_type=MESH)
    for d in range(1, N_LINE):
        pl.semaphore_signal(barrier, inc=1, device_id=at_px(d), device_id_type=MESH)
    for target in others:
        pl.semaphore_signal(barrier, inc=1, device_id={"vert": target}, device_id_type=MESH)

    inputs = [
        pltpu.make_async_copy(source, target, in_sem.at[n])
        for n, (source, target) in enumerate((
            (fac_in, fac), (cs_in, cs), (cov_in, cov), (var_in, var),
            (img, ext.at[:, pl.ds(BORDER, SIDE), :]),
        ))
    ]
    for copy in inputs:
        copy.start()

    inputs[0].wait()
    cells[...] = jnp.zeros((128, 256), f32)
    for v in range(2):
        cells[CELLS * v:CELLS * (v + 1), 0:FACT] = fac[:, v, :]
    for n in range(2):
        slices[4 * n:4 * (n + 1), 0:SLICE] = cells[:, 128 * n:128 * (n + 1)].T.reshape(4, SLICE, 128)
    inputs[1].wait()
    slices[:, SLICE:SLICE + 8] = jnp.full((N_LINE, 8, 128), -1.0, f32)
    for n in range(N_LINE):
        slices[n, SLICE:SLICE + 2, 0:CELLS] = cs[...].astype(f32)
    column[a] = slices[a]

    pl.semaphore_wait(barrier, 2 * (N_LINE - 1) + N_VERT - 1)

    z_copies = [
        remote(
            slices.at[lax.rem(a + d, N_LINE)], column.at[a], zsend.at[d], zrecv.at[N_LINE - d],
            at_py(d),
        )
        for d in FAR_FIRST
    ]
    h_down = remote(
        img.at[:, pl.ds(SIDE - BORDER, BORDER), :], ext.at[:, pl.ds(0, BORDER), :],
        hsend.at[0], hrecv.at[0], at_py(1),
    )
    h_up = remote(
        img.at[:, pl.ds(0, BORDER), :], ext.at[:, pl.ds(BORDER + SIDE, BORDER), :],
        hsend.at[1], hrecv.at[1], at_py(N_LINE - 1),
    )
    for copy in z_copies + [h_down, h_up]:
        copy.start()

    inputs[2].wait()
    inputs[3].wait()

    def weight_rows(r, carry):
        rows = pl.ds(pl.multiple_of(r * CELL, CELL), CELL)
        lane = lanes(CELL)
        for c in range(CPS // 2):
            cols = pl.ds(128 * c, 128)
            total = jnp.zeros((CELL, 128), f32)
            for v in range(2):
                left = cov[v, r * CPS + 2 * c].astype(f32)
                right = cov[v, r * CPS + 2 * c + 1].astype(f32)
                w = jnp.where(lane < CELL, left, right) / var[v, rows, cols]
                weight[v, rows, cols] = w
                total = total + w
            den[rows, cols] = total
            num[rows, cols] = jnp.zeros((CELL, 128), f32)
        return carry

    lax.fori_loop(0, CPS, weight_rows, 0)

    def share(ref, t):
        return ref.at[pl.ds(pl.multiple_of(t * SHARE, SHARE), SHARE)]

    den_copies = [
        remote(share(den, t), rden.at[n], dsend.at[n], drecv.at[n], {"vert": t})
        for n, t in enumerate(others)
    ]
    for copy in den_copies:
        copy.start()

    def share_part(n, first, count, sem):
        t = others[n]
        first = first + lax.rem(t, 2) * (SHARE - count - 2 * first)
        first = pl.multiple_of(first, 32)
        base = pl.multiple_of(t * SHARE + first, 32)
        return remote(
            num.at[pl.ds(base, count)], rnum.at[n, pl.ds(first, count)],
            nsend.at[sem], nrecv.at[sem], {"vert": t},
        )

    for copy in z_copies:
        copy.wait_recv()
    lane = lanes(SLICE)

    def gather_tiles(v):
        for t in range(3):
            tile = jnp.zeros((SLICE, 128), f32)
            for i in range(min(3, N_LINE - 3 * t)):
                inside = (lane >= CELLS * i) & (lane < CELLS * (i + 1))
                part = turn(column[3 * t + i, 0:SLICE], CELLS * (i - v))
                tile = jnp.where(inside, part, tile)
            packed[b, v, :, 128 * t:128 * (t + 1)] = tile

    p_copies = [
        [
            remote(
                packed.at[b, v], packed.at[b, v], psend.at[v, d], precv.at[v, N_LINE - d], at_px(d)
            )
            for d in FAR_FIRST
        ]
        for v in range(2)
    ]
    gather_tiles(0)
    for copy in p_copies[0]:
        copy.start()

    gather_tiles(1)
    for copy in p_copies[1]:
        copy.start()

    names = jnp.concatenate(
        [column[lax.rem(a + d, N_LINE), SLICE:SLICE + 8] for d in range(N_LINE)], axis=0
    )
    wanted = jnp.concatenate([names, names], axis=0).T
    lane = lax.broadcasted_iota(jnp.int32, (1, LINE), 1)
    tile = (lane >= 128).astype(jnp.int32) + (lane >= 256).astype(jnp.int32)
    lane = lane - 128 * tile
    place = (lane >= CELLS).astype(jnp.int32) + (lane >= 2 * CELLS).astype(jnp.int32)
    owner = 3 * tile + place
    stored = owner * (N_LINE * CELLS) + (lane - CELLS * place)
    held = (lane < 3 * CELLS) & (owner < N_LINE)
    stored = jnp.concatenate(
        [jnp.where(held, stored + CELLS * n, -2) for n in range(N_LINE)], axis=1
    ).astype(f32)
    for v in range(2):
        for d in range(0, N_LINE, 2):
            hot[v, PAD * d:PAD * (d + 2)] = jnp.concatenate(
                [
                    jnp.where(wanted[0:PAD, 8 * n + v:8 * n + v + 1] == stored, 1.0, 0.0)
                    for n in (d, d + 1)
                ],
                axis=0,
            ).astype(bf16)

    inputs[4].wait()
    h_down.wait_recv()
    h_up.wait_recv()

    @pl.when(a == 0)
    def _():
        ext[:, 0:BORDER, :] = jnp.zeros((2, BORDER, SIDE), f32)

    @pl.when(a == N_LINE - 1)
    def _():
        ext[:, BORDER + SIDE:ROWS, :] = jnp.zeros((2, BORDER, SIDE), f32)

    def pack(v, carry):
        lane = lanes(CHUNK)
        last = jnp.zeros((CHUNK, 128), f32)
        first = jnp.zeros((CHUNK, 128), f32)
        for g in range(ROWS // CHUNK):
            inside = (lane >= HALF * g) & (lane < HALF * (g + 1))
            rows = slice(CHUNK * g, CHUNK * (g + 1))
            last = jnp.where(inside, turn(ext[v, rows, 256:384], HALF * g - 108), last)
            first = jnp.where(inside, turn(ext[v, rows, 0:128], HALF * g), first)
        xs[0, v] = last
        xs[1, v] = first
        return carry

    lax.fori_loop(0, 2, pack, 0)
    x_copies = [
        remote(xs.at[0], xr.at[0], xsend.at[0], xrecv.at[0], at_px(1)),
        remote(xs.at[1], xr.at[1], xsend.at[1], xrecv.at[1], at_px(N_LINE - 1)),
    ]
    for copy in x_copies:
        copy.start()

    s_copies = [
        [
            remote(
                sbuf.at[v, d], rbuf.at[v, a], ssend.at[v, d], srecv.at[v, N_LINE - d], at_py(d)
            )
            for d in FAR_FIRST
        ]
        for v in range(2)
    ]

    def pick(v):
        for copy in p_copies[v]:
            copy.wait_recv()
        high, low = split(jnp.concatenate([packed[n, v] for n in range(N_LINE)], axis=1))
        table = jnp.concatenate([high, low, jnp.zeros((64, STORE), bf16)], axis=0)
        picked = lax.dot_general(
            hot[v], table, (((1,), (1,)), ((), ())), preferred_element_type=f32
        )
        picked = picked + turn(picked, -SLICE)
        groups = picked.reshape(N_LINE, 5, 8, 128)
        groups = [groups[:, g].reshape(8 * N_LINE, 128) for g in range(5)]
        lane = lanes(8 * N_LINE)
        first = groups[0]
        for g in range(1, 4):
            first = jnp.where(lane < SLICE * g, first, turn(groups[g], SLICE * g))
        sbuf[v, :, 0:8] = first.reshape(N_LINE, 8, 128)
        sbuf[v, :, 8:16] = groups[4].reshape(N_LINE, 8, 128)
        rbuf[v, a] = sbuf[v, 0]
        for copy in s_copies[v]:
            copy.start()

    pick(0)
    pick(1)

    for copy in x_copies:
        copy.wait_recv()

    def tiles(v):
        tall = 2 * CHUNK
        lane = lanes(tall)
        for j in range(ROWS // tall):
            rows = slice(tall * j, tall * (j + 1))
            raw = [ext[v, rows, 128 * d:128 * (d + 1)] for d in range(3)]
            even = [turn(t, HALF) for t in raw]
            odd = [turn(t, 84) for t in raw]
            border = xr[0, v]
            left = jnp.concatenate(
                [turn(border, -HALF * g) for g in (2 * j, 2 * j + 1)], axis=0
            )
            left = jnp.where(b == 0, 0.0, left)
            border = xr[1, v]
            right = jnp.concatenate(
                [turn(border, 84 - HALF * g) for g in (2 * j, 2 * j + 1)], axis=0
            )
            right = jnp.where(b == N_LINE - 1, 0.0, right)
            before = [left] + even
            after = odd + [right]
            for d in range(3):
                high, low = split(jnp.where(lane < HALF, before[d], even[d]))
                thi[v, 2 * d, rows] = high
                tlo[v, 2 * d, rows] = low
                high, low = split(jnp.where(lane < 84, odd[d], after[d + 1]))
                thi[v, 2 * d + 1, rows] = high
                tlo[v, 2 * d + 1, rows] = low

    tiles(0)
    tiles(1)

    half = CELL // 2

    def receive_taps(v):
        for copy in s_copies[v]:
            copy.wait_recv()
        lane = lanes(8)
        total = []
        for n in range(2):
            groups = []
            for g in range(5):
                rows, shift = (slice(0, 8), SLICE * g) if g < 4 else (slice(8, 16), 0)
                piece = turn(rbuf[v, 4 * n, rows], -shift)
                for i in range(1, 4):
                    other = turn(rbuf[v, 4 * n + i, rows], SLICE * i - shift)
                    piece = jnp.where(lane < SLICE * i, piece, other)
                groups.append(piece)
            total.append(jnp.concatenate(groups, axis=0))
        lane = lanes(PAD)
        for p in range(2 * RANK):
            n, offset = divmod(TAPS * p, 128)
            tap = turn(total[n], -offset)
            if offset + TAPS > 128:
                rest = turn(total[n + 1], -offset)
                tap = jnp.where(lane < 128 - offset, tap, rest)
            tap = jnp.where(lane < TAPS, tap, 0.0)
            high = tap.astype(bf16).astype(f32)
            taps[v, p, 0] = high
            taps[v, p, 1] = tap - high

    def band(v, p, part, q, count, shift):
        row = jnp.broadcast_to(taps[v, p, part, pl.ds(q, 1), :], (count, 128))
        return pltpu.roll(row, shift, 1, stride=1, stride_axis=0)

    def row_bands(v, q):
        lane = lanes(half)
        parts = []
        for k in range(RANK):
            near = band(v, 2 * k, 0, q, half, 4)
            low = band(v, 2 * k, 1, q, half, WINDOW + 4)
            far = band(v, 2 * k, 0, q, half, 2 * WINDOW + 4 - 128)
            parts.append(
                jnp.concatenate(
                    [
                        jnp.where(lane < WINDOW, near, low),
                        jnp.where(lane < 2 * WINDOW - 128, low, far),
                    ],
                    axis=1,
                )
            )
        return jnp.concatenate(parts, axis=0).astype(bf16)

    def col_bands(v, q):
        return jnp.concatenate(
            [
                jnp.concatenate(
                    [band(v, 2 * k + 1, part, q, CELL, 0) for k in range(RANK)], axis=1
                )
                for part in range(2)
            ],
            axis=0,
        ).astype(bf16)

    def visit_and_row(step):
        late = step // (2 * EACH)
        visit = (1 - late) * (step // EACH) + late * lax.rem(step, 2)
        place = (1 - late) * lax.rem(step, EACH) + late * (step // 2)
        near = place // 3
        place = place - 3 * near
        flip = lax.rem(x + near, 2)
        place = place + flip * (2 - 2 * place)
        side = x // 2
        return visit, 3 * ((1 - side) * (1 - near) + side * near) + place

    def row_pass(step):
        v, r = visit_and_row(step)
        top = pl.multiple_of(r * CELL, CELL)
        for c in range(CPS):
            windows = []
            for h in range(2):
                rows = pl.ds(pl.multiple_of(top + half * h, half), WINDOW)
                high = thi[v, c, rows, :]
                windows.append(
                    jnp.concatenate([high, high, tlo[v, c, rows, :], high[0:16]], axis=0)
                )
            part = jnp.dot(
                row_bands(v, r * CPS + c), jnp.concatenate(windows, axis=1),
                preferred_element_type=f32,
            )
            halves[lax.rem(step, 2) * CPS + c] = jnp.concatenate(
                [
                    jnp.concatenate(
                        [
                            piece[half * k:half * (k + 1), 128 * h:128 * (h + 1)]
                            for k in range(RANK)
                        ],
                        axis=1,
                    )
                    for piece in split(part)
                    for h in range(2)
                ],
                axis=0,
            )

    def col_pass(step):
        v, r = visit_and_row(step)
        rows = pl.ds(pl.multiple_of(r * CELL, CELL), CELL)
        for c in range(0, CPS, 2):
            pair = []
            for n in (c, c + 1):
                both = lax.dot_general(
                    halves[lax.rem(step, 2) * CPS + n], col_bands(v, r * CPS + n),
                    (((1,), (1,)), ((), ())), preferred_element_type=f32,
                )
                both = both[0:CELL] + both[CELL:2 * CELL]
                pair.append(both + turn(both, CELL))
            cols = slice(CELL * c, CELL * c + 128)
            term = weight[v, rows, cols] * jnp.where(lanes(CELL) < CELL, pair[0], pair[1])
            num[rows, cols] = num[rows, cols] + term

    num_copies = [
        share_part(0, 0, 64, 0), share_part(0, 64, 32, 1), share_part(1, 0, 96, 2),
        share_part(2, 0, 64, 3), share_part(2, 64, 32, 4),
    ]

    receive_taps(0)
    row_pass(jnp.int32(0))

    @pl.loop(1, EACH)
    def _(step):
        row_pass(step)
        col_pass(step - 1)

    receive_taps(1)

    @pl.loop(EACH, 2 * CPS)
    def _(step):
        row_pass(step)
        col_pass(step - 1)
        for copy, ready in zip(num_copies, (6, 7, 8, 9, 10)):

            @pl.when(step == ready)
            def _():
                copy.start()

    col_pass(jnp.int32(2 * CPS - 1))

    mine = pl.ds(pl.multiple_of(x * SHARE, SHARE), SHARE)
    for copy in den_copies + num_copies:
        copy.wait_recv()
    weight_sum[...] = (den[mine] + rden[1]) + (rden[0] + rden[2])
    top_sum[...] = (num[mine] + rnum[1]) + (rnum[0] + rnum[2])

    for copy in z_copies + [h_down, h_up] + x_copies + p_copies[0] + p_copies[1]:
        copy.wait_send()
    for copy in s_copies[0] + s_copies[1] + den_copies + num_copies:
        copy.wait_send()


def shards(warped_image, variance, kernel_factors, cell_source, coverage):
    vmem = pl.BlockSpec(memory_space=pltpu.VMEM)
    dma = pltpu.SemaphoreType.DMA
    out = jax.ShapeDtypeStruct((SHARE, SIDE), f32)
    top_sum, weight_sum = pl.pallas_call(
        kernel,
        out_shape=(out, out),
        in_specs=[pl.BlockSpec(memory_space=pl.ANY)] * 5,
        out_specs=(vmem, vmem),
        scratch_shapes=[
            pltpu.VMEM((2, ROWS, SIDE), f32),
            pltpu.VMEM((2, SIDE, SIDE), f32),
            pltpu.VMEM((CELLS, 2, FACT), f32),
            pltpu.VMEM((2, CELLS), jnp.int32),
            pltpu.SMEM((2, CELLS), jnp.int32),
            pltpu.VMEM((128, 256), f32),
            pltpu.VMEM((N_LINE, SLICE + 8, 128), f32),
            pltpu.VMEM((N_LINE, SLICE + 8, 128), f32),
            pltpu.VMEM((N_LINE, 2, SLICE, LINE), f32),
            pltpu.VMEM((2, N_LINE * PAD, STORE), bf16),
            pltpu.VMEM((2, N_LINE, 16, 128), f32),
            pltpu.VMEM((2, N_LINE, 16, 128), f32),
            pltpu.VMEM((2, 2 * RANK, 2, PAD, 128), f32),
            pltpu.VMEM((2, 2, CHUNK, 128), f32),
            pltpu.VMEM((2, 2, CHUNK, 128), f32),
            pltpu.VMEM((2, CPS, ROWS, 128), bf16),
            pltpu.VMEM((2, CPS, ROWS, 128), bf16),
            pltpu.VMEM((2, SIDE, SIDE), f32),
            pltpu.VMEM((SIDE, SIDE), f32),
            pltpu.VMEM((SIDE, SIDE), f32),
            pltpu.VMEM((N_VERT - 1, SHARE, SIDE), f32),
            pltpu.VMEM((N_VERT - 1, SHARE, SIDE), f32),
            pltpu.VMEM((2 * CPS, 128, 384), bf16),
            dma((5,)),
            dma((N_LINE,)), dma((N_LINE,)),
            dma((2, N_LINE)), dma((2, N_LINE)),
            dma((2, N_LINE)), dma((2, N_LINE)),
            dma((2,)), dma((2,)), dma((2,)), dma((2,)),
            dma((5,)), dma((5,)), dma((3,)), dma((3,)),
        ],
        compiler_params=pltpu.CompilerParams(
            collective_id=0, has_side_effects=True, vmem_limit_bytes=60 * 1024 * 1024
        ),
    )(warped_image, variance, kernel_factors.transpose(1, 0, 2), cell_source, coverage)
    weight_sum = jnp.maximum(weight_sum, 0.5)
    return top_sum / weight_sum, weight_sum


def solution(mesh):
    placed = (
        P("vert", "py", "px"),
        P("vert", "py", "px"),
        P("vert", ("py", "px"), None),
        P("vert", ("py", "px")),
        P("vert", ("py", "px")),
    )
    return jax.shard_map(
        shards,
        mesh=mesh,
        in_specs=placed,
        out_specs=(P(("py", "vert"), "px"), P(("py", "vert"), "px")),
        check_vma=False,
    )
```
